128 devices in a mesh: view: 8 (over x, core), depth: 16 (over y, z).
Axes of the slice: x: 4, y: 4, z: 4, core: 2. Of those that a mesh axis runs over, the one named last changes fastest.
Arguments:
- features: float32 [8, 16, 32, 3, 4096], P('view', 'depth'), may hold values from -6 to 6
- spacing: float32 [8, 16, 3, 4096], P('view', 'depth'), may hold values from 0.01 to 0.15
- counts: int32 [8, 16, 4096], P('view', 'depth'), may hold values from 0 to 3
- depth_rank: int32 [8, 16], P('view', 'depth'), may hold values from 0 to 15, as said below
- target: float32 [8, 64, 4096], P('view', None, 'depth'), may hold values from 0 to 1
- first_weight: float32 [32, 256], replicated, may hold values from -1 to 1
- first_bias: float32 [256], replicated, may hold values from -3 to 3
- second_weight: float32 [256, 256], replicated, may hold values from -0.375 to 0.375
- second_bias: float32 [256], replicated, may hold values from -3 to 3
- last_weight: float32 [256, 65], replicated, may hold values from -0.375 to 0.375
- last_bias: float32 [65], replicated, may hold values from -3 to 3
Outputs:
- pixels: float32 [8, 64, 4096], P('view', None, 'depth')
- first_update: float32 [32, 256], replicated
- first_shift: float32 [256], replicated
- second_update: float32 [256, 256], replicated
- second_shift: float32 [256], replicated
- last_update: float32 [256, 65], replicated
- last_shift: float32 [65], replicated
The draws below stay inside these ranges and needn't reach their ends.
Inputs may be any that keep to these rules, and one draw needn't show every extreme that they name: depth_rank[v, d] equals d XOR a number fixed for view group v, so each view group's ranks are a permutation in which every aligned block of 2^k regions takes consecutive positions. Sample slots s with s < counts[v, d, r] are live.
All inputs are finite; a program needn't handle non-finite values.
Results may differ from the reference program's by a relative error of at most 0.0003.
Values sent between devices are 32-bit elements; how exact they have to be, the bound alone decides.
No kernel may reach another device: no remote copies, remote signals or barrier semaphores. Data moves between devices by JAX's collectives and lax.ppermute only.
A program may use at most 128 MiB of HBM per device.

```python
import math
import jax
import jax.numpy as jnp
from jax import lax

FEAT = 32
HIDDEN_SIZE = 256
CHANNELS = 64
SAMPLES = 3
RAYS = 4096
OUT = 65
VIEWS = 8
REGIONS = 16


def draw_depth_rank(key, part):
    region_ids = jnp.arange(REGIONS, dtype=jnp.int32)
    flips = jax.random.randint(jax.random.fold_in(key, 17), (VIEWS, 1), 0, REGIONS).astype(jnp.int32)
    return jnp.bitwise_xor(region_ids[None, :], flips).astype(jnp.int32)


def plant(entries, key, low, high):
    longest = entries.shape.index(max(entries.shape))
    spots = []
    for shift in (0, 1):
        where = [jax.random.randint(jax.random.fold_in(key, axis), (), 0, length) for axis, length in enumerate(entries.shape)]
        where[longest] = (where[longest] + shift) % entries.shape[longest]
        spots.append(tuple(where))
    return entries.at[spots[0]].set(low).at[spots[1]].set(high)


def block_scale(rng, extent, shards, low, high):
    gain = 1.0
    for dim, shards_of in shards:
        steps = jax.random.uniform(jax.random.fold_in(jax.random.fold_in(rng, 6), dim), (shards_of,), jnp.float32, low / len(shards), high / len(shards))
        gain = gain * jnp.repeat(jnp.exp(steps), extent[dim] // shards_of).reshape((-1,) + (1,) * (len(extent) - 1 - dim))
    return gain


def normal_values(own_key, shape, deviation, most, pieces=(), kind=jnp.bfloat16):
    entries = jax.random.normal(own_key, shape, jnp.float32) * deviation
    if len(pieces) > 0:
        entries = block_scale(own_key, shape, pieces, -0.22, 0.18) * entries
    return jnp.clip(entries, min=-most, max=most).astype(kind)


def setup_inputs(seed: int = 0) -> dict:
    key_of = jax.random.split(jax.random.key(seed), 12)
    features = normal_values(key_of[0], (VIEWS, REGIONS, FEAT, SAMPLES, RAYS), 1.0, 6.0, ((0, 8), (1, 16)), jnp.float32)
    spacing = jnp.clip(jnp.exp(math.log(0.15) - 2.7080503 * jax.random.uniform(key_of[1], (VIEWS, REGIONS, SAMPLES, RAYS), jnp.float32) ** block_scale(key_of[1], (VIEWS, REGIONS, SAMPLES, RAYS), ((0, 8), (1, 16)), -0.2, 0.2)), 0.01, 0.15)
    counts = plant(jax.random.randint(key_of[2], (VIEWS, REGIONS, RAYS), 0, SAMPLES + 1), jax.random.fold_in(key_of[2], 1), 0, SAMPLES).astype(jnp.int32)
    depth_rank = draw_depth_rank(jax.random.fold_in(key_of[11], 71), 0)
    target = jnp.clip(1.0 * jax.random.uniform(key_of[4], (VIEWS, CHANNELS, RAYS), jnp.float32) ** block_scale(key_of[4], (VIEWS, CHANNELS, RAYS), ((0, 8), (2, 16)), -0.2, 0.2), 0.0, 1.0)
    first_weight = normal_values(key_of[5], (FEAT, HIDDEN_SIZE), FEAT ** -0.5, 1.0, (), jnp.float32)
    first_bias = normal_values(key_of[6], (HIDDEN_SIZE,), 0.5, 3.0, (), jnp.float32)
    second_weight = normal_values(key_of[7], (HIDDEN_SIZE, HIDDEN_SIZE), HIDDEN_SIZE ** -0.5, 0.375, (), jnp.float32)
    second_bias = normal_values(key_of[8], (HIDDEN_SIZE,), 0.5, 3.0, (), jnp.float32)
    last_weight = normal_values(key_of[9], (HIDDEN_SIZE, OUT), HIDDEN_SIZE ** -0.5, 0.375, (), jnp.float32)
    last_bias = normal_values(key_of[10], (OUT,), 0.5, 3.0, (), jnp.float32)
    return {"features": features, "spacing": spacing, "counts": counts, "depth_rank": depth_rank, "target": target, "first_weight": first_weight, "first_bias": first_bias, "second_weight": second_weight, "second_bias": second_bias, "last_weight": last_weight, "last_bias": last_bias}


precise = lax.Precision.HIGHEST
epsilon = 1e-05

def project(weight, inputs):
    return lax.dot_general(weight, inputs, (((0,), (0,)), ((), ())), precision=precise, preferred_element_type=jnp.float32)

def render(params, sample_feats, sample_spacing, live_mask):
    first_weight, first_bias, second_weight, second_bias, last_weight, last_bias = params
    columns = sample_feats.reshape(sample_feats.shape[0], -1)
    first_act = jax.nn.relu(project(first_weight, columns) + first_bias[:, None])
    second_act = jax.nn.relu(project(second_weight, first_act) + second_bias[:, None])
    raw_output = project(last_weight, second_act) + last_bias[:, None]
    raw_output = raw_output.reshape(raw_output.shape[0], sample_spacing.shape[0], sample_spacing.shape[1])
    channels = raw_output.shape[0] - 1
    sample_color = jax.nn.sigmoid(raw_output[:channels])
    density = jax.nn.softplus(raw_output[channels])
    optical = density * sample_spacing * live_mask
    before = jnp.cumsum(optical, axis=0) - optical
    weight = jnp.exp(-before) * (1.0 - jnp.exp(-optical))
    region_color = lax.optimization_barrier(jnp.sum(weight[None] * sample_color, axis=1))
    region_depth = lax.optimization_barrier(jnp.sum(optical, axis=0))
    return (region_color, region_depth)

def normalize(gradient):
    return gradient / jnp.sqrt(jnp.mean(gradient * gradient) + epsilon)

def reference(features, spacing, counts, depth_rank, target, first_weight, first_bias, second_weight, second_bias, last_weight, last_bias):
    params = (first_weight, first_bias, second_weight, second_bias, last_weight, last_bias)
    sample_ids = jnp.arange(SAMPLES, dtype=jnp.int32)
    live_mask = (sample_ids[None, None, :, None] < counts[:, :, None, :]).astype(jnp.float32)
    flat_feats = features.reshape(VIEWS * REGIONS, FEAT, SAMPLES, RAYS)
    flat_spacing = spacing.reshape(VIEWS * REGIONS, SAMPLES, RAYS)
    flat_live = live_mask.reshape(VIEWS * REGIONS, SAMPLES, RAYS)

    def forward(scan_items):
        return render(params, scan_items[0], scan_items[1], scan_items[2])
    colors, depths = lax.map(forward, (flat_feats, flat_spacing, flat_live))
    colors = colors.reshape(VIEWS, REGIONS, CHANNELS, RAYS)
    depths = depths.reshape(VIEWS, REGIONS, RAYS)
    earlier = (depth_rank[:, None, :] < depth_rank[:, :, None]).astype(jnp.float32)
    later_mask = (depth_rank[:, None, :] > depth_rank[:, :, None]).astype(jnp.float32)
    passed = jnp.exp(-jnp.einsum('vde,ver->vdr', earlier, depths, precision=precise))
    weighted = passed[:, :, None, :] * colors
    pixels = lax.optimization_barrier(jnp.sum(weighted, axis=1))
    misfit = pixels - target
    color_grad = passed[:, :, None, :] * misfit[:, None]
    behind = jnp.einsum('vde,vecr->vdcr', later_mask, weighted, precision=precise)
    depth_grad = -lax.optimization_barrier(jnp.sum(misfit[:, None] * behind, axis=2))

    def accumulate(running, scan_items):
        sample_feats, sample_spacing, live_part, color_part, depth_part = scan_items
        unused, pullback = jax.vjp(lambda weights: render(weights, sample_feats, sample_spacing, live_part), params)
        gradients = pullback((color_part, depth_part))[0]
        return (jax.tree.map(jnp.add, running, gradients), None)
    zero_grads = jax.tree.map(jnp.zeros_like, params)
    totals, unused_out = lax.scan(accumulate, zero_grads, (flat_feats, flat_spacing, flat_live, color_grad.reshape(VIEWS * REGIONS, CHANNELS, RAYS), depth_grad.reshape(VIEWS * REGIONS, RAYS)))
    return (pixels, normalize(totals[0]), normalize(totals[1]), normalize(totals[2]), normalize(totals[3]), normalize(totals[4]), normalize(totals[5]))
```

```python
import functools

import jax
import jax.numpy as jnp
from jax import lax
from jax.experimental import pallas as pl
from jax.experimental.pallas import tpu as pltpu
from jax.sharding import PartitionSpec as P

epsilon = 1e-05
f32 = jnp.float32
bf16 = jnp.bfloat16
FEAT, HIDDEN, CHANNELS, SAMPLES = 32, 256, 64, 3
OUT_ROWS = 80
ONES = 16


def split(value):
    high = value.astype(bf16)
    return high, (value - high.astype(f32)).astype(bf16)


def dot(left, right):
    return lax.dot_general(left, right, (((1,), (0,)), ((), ())), preferred_element_type=f32)


def dot_columns(left, right):
    return lax.dot_general(left, right, (((1,), (1,)), ((), ())), preferred_element_type=f32)


def sigmoid(value):
    return 0.5 * jnp.tanh(0.5 * value) + 0.5


def step_kernel(
    flip_ref,
    rays_ref,
    target_ref,
    first_t_ref,
    first_bias_ref,
    second_ref,
    second_t_ref,
    second_bias_ref,
    last_ref,
    last_t_ref,
    last_bias_ref,
    pixels_ref,
    grads_ref,
    first_k,
    second_h,
    second_l,
    second_th,
    second_tl,
    last_k,
    last_thl,
    act1_h,
    act1_l,
    act2_h,
    act2_l,
    colors,
    rows,
    misfit_ref,
    grad1,
    grad2,
    grad3,
    bias3,
):
    regions, _, segment = rays_ref.shape
    flip = flip_ref[0]
    columns = SAMPLES * segment

    high, low = split(first_t_ref[...])
    bias_h = first_bias_ref[...].astype(bf16)
    rest = first_bias_ref[...] - bias_h.astype(f32)
    bias_m = rest.astype(bf16)
    bias_l = (rest - bias_m.astype(f32)).astype(bf16)
    pad = jnp.zeros((HIDDEN, ONES - 3), bf16)
    first_k[...] = jnp.concatenate([high, high, low, bias_h, bias_m, bias_l, pad], axis=1)
    high, low = split(second_ref[...])
    second_h[...] = high
    second_l[...] = low
    high, low = split(second_t_ref[...])
    second_th[...] = high
    second_tl[...] = low
    high, low = split(last_ref[...])
    last_k[...] = jnp.concatenate([high, high, low], axis=1)
    high, low = split(last_t_ref[...])
    last_thl[...] = jnp.concatenate([high, low], axis=0)
    grad1[...] = jnp.zeros_like(grad1)
    grad2[...] = jnp.zeros_like(grad2)
    grad3[...] = jnp.zeros_like(grad3)
    bias3[...] = jnp.zeros_like(bias3)
    misfit_ref[...] = jnp.zeros_like(misfit_ref)
    ones = jnp.ones((ONES, columns), bf16)

    def part(value, s):
        return value[:, s * segment : (s + 1) * segment]

    def inputs(d):
        x = jnp.concatenate([rays_ref[d, s * FEAT : (s + 1) * FEAT, :] for s in range(SAMPLES)], axis=1)
        return split(x)

    def forward(position, cum):
        d = jnp.bitwise_xor(position, flip)
        xh, xl = inputs(d)
        a1 = jnp.maximum(dot(first_k[...], jnp.concatenate([xh, xl, xh, ones], axis=0)), 0.0)
        a1h, a1l = split(a1)
        act1_h[d, :HIDDEN] = a1h
        act1_h[d, HIDDEN:] = ones
        act1_l[d] = a1l
        z2 = dot(second_th[...], a1h) + (dot(second_tl[...], a1h) + dot(second_th[...], a1l))
        a2 = jnp.maximum(z2 + second_bias_ref[...], 0.0)
        a2h, a2l = split(a2)
        act2_h[d] = a2h
        act2_l[d] = a2l
        both = dot(last_thl[...], a2h)
        raw = both[:OUT_ROWS] + (both[OUT_ROWS:] + dot(last_thl[:OUT_ROWS], a2l)) + last_bias_ref[...]
        sc = sigmoid(raw[:CHANNELS])
        colors[d] = sc
        t = raw[CHANNELS : CHANNELS + 1]
        density = jnp.maximum(t, 0.0) + jnp.log1p(jnp.exp(-jnp.abs(t)))
        slope = sigmoid(t)
        passed = jnp.exp(-cum)
        before = jnp.ones_like(cum)
        total = jnp.zeros_like(cum)
        color = jnp.zeros((CHANNELS, segment), f32)
        for s in range(SAMPLES):
            length = rays_ref[d, SAMPLES * FEAT + s : SAMPLES * FEAT + s + 1, :]
            optical = part(density, s) * length
            weight = before * (1.0 - jnp.exp(-optical))
            total = total + optical
            before = jnp.exp(-total)
            color = color + weight * part(sc, s)
            rows[d, s : s + 1, :] = weight
            rows[d, SAMPLES + s : SAMPLES + s + 1, :] = before
            rows[d, 2 * SAMPLES + s : 2 * SAMPLES + s + 1, :] = part(slope, s) * length
        rows[d, 9:10, :] = passed
        misfit_ref[...] += passed * color
        return cum + total

    lax.fori_loop(0, regions, forward, jnp.zeros((1, segment), f32))
    pixels = misfit_ref[...]
    pixels_ref[...] = pixels
    misfit_ref[...] = pixels - target_ref[...]

    def backward(step, behind):
        d = jnp.bitwise_xor(regions - 1 - step, flip)
        misfit = misfit_ref[...]
        passed = rows[d, 9:10, :]
        weights = [rows[d, s : s + 1, :] for s in range(SAMPLES)]
        parts, weighted, dots = [], [], []
        for s in range(SAMPLES):
            sc = colors[d, :, s * segment : (s + 1) * segment]
            product = misfit * sc
            value = passed * jnp.sum(product, axis=0, keepdims=True)
            dots.append(value)
            weighted.append(weights[s] * value)
            parts.append((passed * weights[s]) * (product - product * sc))
        later = -behind
        slopes = [None] * SAMPLES
        for s in reversed(range(SAMPLES)):
            after = rows[d, SAMPLES + s : SAMPLES + s + 1, :]
            slopes[s] = (dots[s] * after + later) * rows[d, 2 * SAMPLES + s : 2 * SAMPLES + s + 1, :]
            later = later - weighted[s]
        d3 = jnp.concatenate(
            [
                jnp.concatenate(parts, axis=1),
                jnp.concatenate(slopes, axis=1),
                jnp.zeros((OUT_ROWS - CHANNELS - 1, columns), f32),
            ],
            axis=0,
        )
        bias3[...] += part(d3, 0) + (part(d3, 1) + part(d3, 2))
        d3h, d3l = split(d3)
        a2h = act2_h[d]
        d2 = dot(last_k[...], jnp.concatenate([d3h, d3l, d3h], axis=0))
        d2 = jnp.where(a2h > 0, d2, 0.0)
        d2h, d2l = split(d2)
        both = dot_columns(jnp.concatenate([d3h, d3l], axis=0), a2h)
        grad3[...] += both[:OUT_ROWS] + (both[OUT_ROWS:] + dot_columns(d3h, act2_l[d]))
        a1h = act1_h[d]
        d1 = dot(second_h[...], d2h) + (dot(second_l[...], d2h) + dot(second_h[...], d2l))
        d1 = jnp.where(a1h[:HIDDEN] > 0, d1, 0.0)
        grad2[...] += dot_columns(a1h, d2h) + dot_columns(a1h, d2l)
        grad2[:HIDDEN] += dot_columns(act1_l[d], d2h)
        d1h, d1l = split(d1)
        xh, xl = inputs(d)
        both = dot_columns(jnp.concatenate([xh, ones, xl], axis=0), d1h)
        other = dot_columns(jnp.concatenate([xh, ones], axis=0), d1l)
        grad1[...] += both[: FEAT + ONES] + other
        grad1[:FEAT] += both[FEAT + ONES :]
        return behind + (weighted[0] + (weighted[1] + weighted[2]))

    lax.fori_loop(0, regions, backward, jnp.zeros((1, segment), f32))

    half = HIDDEN // 2
    third = lax.dot_general(
        jnp.ones((8, segment), f32),
        jnp.concatenate([bias3[...], jnp.zeros((half - OUT_ROWS, segment), f32)], axis=0),
        (((1,), (1,)), ((), ())),
        precision=lax.Precision.HIGHEST,
        preferred_element_type=f32,
    )
    grads_ref[...] = jnp.zeros_like(grads_ref)
    for side in range(2):
        lanes = slice(side * half, (side + 1) * half)
        grads_ref[side * 256 : side * 256 + 256] = grad2[:HIDDEN, lanes]
        grads_ref[512 + side * 32 : 544 + side * 32] = grad1[:FEAT, lanes]
        grads_ref[576 + side * 80 : 656 + side * 80] = grad3[:, lanes]
        grads_ref[736 + side * 8 : 737 + side * 8] = grad1[FEAT : FEAT + 1, lanes]
        grads_ref[737 + side * 8 : 738 + side * 8] = grad2[HIDDEN : HIDDEN + 1, lanes]
    grads_ref[738:739] = third[0:1]


def finish_kernel(sums_ref, first_ref, first_b_ref, second_ref, second_b_ref, last_ref, last_b_ref):
    def scale(parts, count):
        squares = sum(jnp.sum(part * part, keepdims=True) for part in parts)
        return 1.0 / jnp.sqrt(squares / count + epsilon)

    def both(start, rows, stride):
        return [sums_ref[start : start + rows, :], sums_ref[start + stride : start + stride + rows, :]]

    parts = both(0, 256, 256)
    second_ref[...] = jnp.concatenate(parts, axis=1) * scale(parts, HIDDEN * HIDDEN)
    parts = both(512, 32, 32)
    first_ref[...] = jnp.concatenate(parts, axis=1) * scale(parts, FEAT * HIDDEN)
    parts = both(576, 80, 80)
    last = jnp.concatenate(parts, axis=1) * scale(parts, HIDDEN * (CHANNELS + 1))
    last = jnp.concatenate([last, jnp.zeros((128 - OUT_ROWS, HIDDEN), f32)], axis=0)
    last_ref[...] = jnp.transpose(last)[:, : CHANNELS + 1]
    parts = both(736, 1, 8)
    first_b_ref[...] = jnp.concatenate(parts, axis=1) * scale(parts, HIDDEN)
    parts = both(737, 1, 8)
    second_b_ref[...] = jnp.concatenate(parts, axis=1) * scale(parts, HIDDEN)
    part = sums_ref[738:739, :]
    last_b_ref[...] = (part * scale([part], CHANNELS + 1))[:, : CHANNELS + 1]


def local(
    features,
    spacing,
    counts,
    depth_rank,
    target,
    first_weight,
    first_bias,
    second_weight,
    second_bias,
    last_weight,
    last_bias,
):
    regions = lax.axis_size("depth")
    devices = regions * lax.axis_size("view")
    rays = features.shape[-1]
    segment = rays // regions
    flip = jnp.bitwise_xor(depth_rank[0, 0], lax.axis_index("depth")).reshape(1)

    sample_ids = jnp.arange(SAMPLES, dtype=jnp.int32)
    length = jnp.where(sample_ids[:, None] < counts[0, 0][None, :], spacing[0, 0], 0.0)
    sent = jnp.concatenate(
        [
            features[0, 0].transpose(1, 0, 2).reshape(SAMPLES * FEAT, rays),
            length,
            jnp.zeros((8 - SAMPLES, rays), f32),
        ],
        axis=0,
    )
    height = sent.shape[0]
    sent = sent.reshape(height, regions, segment).transpose(1, 0, 2)
    got = lax.all_to_all(sent, "depth", 0, 0)

    last_pad = jnp.pad(last_weight, ((0, 0), (0, OUT_ROWS - CHANNELS - 1)))
    columns = SAMPLES * segment
    vmem = pl.BlockSpec(memory_space=pltpu.VMEM)
    pixels, grads = pl.pallas_call(
        step_kernel,
        in_specs=[pl.BlockSpec(memory_space=pltpu.SMEM)] + [vmem] * 10,
        out_specs=[vmem] * 2,
        out_shape=[
            jax.ShapeDtypeStruct((CHANNELS, segment), f32),
            jax.ShapeDtypeStruct((1024, 128), f32),
        ],
        scratch_shapes=[
            pltpu.VMEM((HIDDEN, 3 * FEAT + ONES), bf16),
            pltpu.VMEM((HIDDEN, HIDDEN), bf16),
            pltpu.VMEM((HIDDEN, HIDDEN), bf16),
            pltpu.VMEM((HIDDEN, HIDDEN), bf16),
            pltpu.VMEM((HIDDEN, HIDDEN), bf16),
            pltpu.VMEM((HIDDEN, 3 * OUT_ROWS), bf16),
            pltpu.VMEM((2 * OUT_ROWS, HIDDEN), bf16),
            pltpu.VMEM((regions, HIDDEN + ONES, columns), bf16),
            pltpu.VMEM((regions, HIDDEN, columns), bf16),
            pltpu.VMEM((regions, HIDDEN, columns), bf16),
            pltpu.VMEM((regions, HIDDEN, columns), bf16),
            pltpu.VMEM((regions, CHANNELS, columns), f32),
            pltpu.VMEM((regions, 16, segment), f32),
            pltpu.VMEM((CHANNELS, segment), f32),
            pltpu.VMEM((FEAT + ONES, HIDDEN), f32),
            pltpu.VMEM((HIDDEN + ONES, HIDDEN), f32),
            pltpu.VMEM((OUT_ROWS, HIDDEN), f32),
            pltpu.VMEM((OUT_ROWS, segment), f32),
        ],
        compiler_params=pltpu.CompilerParams(vmem_limit_bytes=52 * 2**20),
        cost_estimate=pl.CostEstimate(
            flops=2 * 17 * 65536 * regions * columns, bytes_accessed=4 * 2**20, transcendentals=0
        ),
    )(
        flip,
        got,
        target[0],
        first_weight.T,
        first_bias[:, None],
        second_weight,
        second_weight.T,
        second_bias[:, None],
        last_pad,
        last_pad.T,
        jnp.pad(last_bias, (0, OUT_ROWS - CHANNELS - 1))[:, None],
    )

    axes = ("view", "depth")
    shares = lax.all_to_all(grads.reshape(devices, 1024 // devices, 128), axes, 0, 0)
    share = jnp.sum(shares, axis=0)
    sums = lax.all_to_all(jnp.broadcast_to(share[None], shares.shape), axes, 0, 0)
    first_u, first_s, second_u, second_s, last_u, last_s = pl.pallas_call(
        finish_kernel,
        in_specs=[vmem],
        out_specs=[vmem] * 6,
        out_shape=[
            jax.ShapeDtypeStruct((FEAT, HIDDEN), f32),
            jax.ShapeDtypeStruct((1, HIDDEN), f32),
            jax.ShapeDtypeStruct((HIDDEN, HIDDEN), f32),
            jax.ShapeDtypeStruct((1, HIDDEN), f32),
            jax.ShapeDtypeStruct((HIDDEN, CHANNELS + 1), f32),
            jax.ShapeDtypeStruct((1, CHANNELS + 1), f32),
        ],
    )(sums.reshape(1024, 128))
    return (pixels[None], first_u, first_s[0], second_u, second_s[0], last_u, last_s[0])


def solution(mesh):
    return jax.shard_map(
        local,
        mesh=mesh,
        in_specs=(
            P("view", "depth", None, None, None),
            P("view", "depth", None, None),
            P("view", "depth", None),
            P("view", "depth"),
            P("view", None, "depth"),
            P(),
            P(),
            P(),
            P(),
            P(),
            P(),
        ),
        out_specs=(P("view", None, "depth"), P(), P(), P(), P(), P(), P()),
        check_vma=False,
    )
```

```python
import functools

import jax
import jax.numpy as jnp
from jax import lax
from jax.experimental import pallas as pl
from jax.experimental.pallas import tpu as pltpu
from jax.sharding import PartitionSpec as P

epsilon = 1e-05
f32 = jnp.float32
bf16 = jnp.bfloat16
FEAT, HIDDEN, CHANNELS, SAMPLES = 32, 256, 64, 3
OUT = CHANNELS + 1
OUT_ROWS = 80
ONES = 16
HEIGHT = 104
PARTS = 2
TOGETHER = 4
UNROLL = 1
PACKED = 1024


def split(value):
    high = value.astype(bf16)
    return high, (value - high.astype(f32)).astype(bf16)


def dot(left, right):
    return lax.dot_general(left, right, (((1,), (0,)), ((), ())), preferred_element_type=f32)


def dot_columns(left, right):
    return lax.dot_general(left, right, (((1,), (1,)), ((), ())), preferred_element_type=f32)


def sigmoid(value):
    return 0.5 * jnp.tanh(0.5 * value) + 0.5


def send_kernel(features_ref, spacing_ref, counts_ref, *sent_refs):
    regions = sent_refs[0].shape[0]
    parts = len(sent_refs)
    lanes = sent_refs[0].shape[2]
    lengths = [
        jnp.where(counts_ref[...] > s, spacing_ref[s], 0.0) for s in range(SAMPLES)
    ]
    wide = lanes // 128
    for j in range(regions):
        for i, sent_ref in enumerate(sent_refs):
            start = (j * parts + i) * lanes
            sent_ref[j, : SAMPLES * FEAT, :] = features_ref[:, start : start + lanes]
            row = (j * parts + i) * wide
            for k in range(wide):
                sent_ref[j, SAMPLES * FEAT :, k * 128 : (k + 1) * 128] = jnp.concatenate(
                    [v[row + k : row + k + 1] for v in lengths]
                    + [jnp.zeros((HEIGHT - SAMPLES * FEAT - SAMPLES, 128), f32)],
                    axis=0,
                )


def weights_kernel(
    first_ref,
    first_bias_ref,
    second_ref,
    second_bias_ref,
    last_t_ref,
    last_bias_ref,
    first_k,
    second_k,
    second_tk,
    second_b,
    last_k,
    last_thl,
    last_b,
):
    def column(row, size):
        return jnp.transpose(jnp.broadcast_to(row, (8, size)))[:, 0:1]

    high, low = split(jnp.transpose(first_ref[...]))
    bias = column(first_bias_ref[...], HIDDEN)
    bias_h = bias.astype(bf16)
    rest = bias - bias_h.astype(f32)
    bias_m = rest.astype(bf16)
    bias_l = (rest - bias_m.astype(f32)).astype(bf16)
    pad = jnp.zeros((HIDDEN, ONES - 3), bf16)
    first_k[...] = jnp.concatenate([high, high, low, bias_h, bias_m, bias_l, pad], axis=1)
    high, low = split(second_ref[...])
    second_k[...] = jnp.concatenate([high, low, high], axis=1)
    high, low = split(jnp.transpose(second_ref[...]))
    second_tk[...] = jnp.concatenate([high, low, high], axis=1)
    second_b[...] = column(second_bias_ref[...], HIDDEN)
    last_t = jnp.concatenate([last_t_ref[...], jnp.zeros((128 - OUT, HIDDEN), f32)], axis=0)
    high, low = split(last_t[:OUT_ROWS])
    last_thl[...] = jnp.concatenate([high, low], axis=0)
    high, low = split(jnp.transpose(last_t)[:, :OUT_ROWS])
    last_k[...] = jnp.concatenate([high, high, low], axis=1)
    row = jnp.concatenate([last_bias_ref[...], jnp.zeros((1, 128 - OUT), f32)], axis=1)
    last_b[...] = column(row, 128)[:OUT_ROWS]


def step_kernel(first, final, flip_ref, rays_ref, target_ref, *refs):
    first_k, second_k, second_tk, second_b, last_k, last_thl, last_b = refs[:7]
    refs = refs[7:]
    if not first:
        pixels_in, grad1_in, grad2_in, grad3_in, bias3_in = refs[:5]
        refs = refs[5:]
    if final:
        pixels_ref, grads_ref = refs[:2]
        grad1, grad2, grad3, bias3 = refs[2:6]
        refs = refs[6:]
    else:
        pixels_ref, grad1, grad2, grad3, bias3 = refs[:5]
        refs = refs[5:]
    act1_h, act1_l, act2_h, act2_l, colors, rows, misfit_ref = refs
    regions, _, segment = rays_ref.shape
    flip = flip_ref[0]
    pieces = [(g, s) for g in range(TOGETHER) for s in range(SAMPLES)]
    columns = len(pieces) * segment

    if first:
        grad1[...] = jnp.zeros_like(grad1)
        grad2[...] = jnp.zeros_like(grad2)
        grad3[...] = jnp.zeros_like(grad3)
        bias3[...] = jnp.zeros_like(bias3)
    else:
        grad1[...] = grad1_in[...]
        grad2[...] = grad2_in[...]
        grad3[...] = grad3_in[...]
        bias3[...] = bias3_in[...]
    misfit_ref[...] = jnp.zeros_like(misfit_ref)
    ones = jnp.ones((ONES, columns), bf16)

    def part(value, g, s):
        start = (g * SAMPLES + s) * segment
        return value[:, start : start + segment]

    def region(step, g):
        return jnp.bitwise_xor(step * TOGETHER + g, flip)

    def inputs(step):
        x = [rays_ref[region(step, g), s * FEAT : (s + 1) * FEAT, :] for g, s in pieces]
        return split(jnp.concatenate(x, axis=1))

    def forward(step, cum):
        xh, xl = inputs(step)
        a1 = jnp.maximum(dot(first_k[...], jnp.concatenate([xh, xl, xh, ones], axis=0)), 0.0)
        a1h, a1l = split(a1)
        act1_h[step, :HIDDEN] = a1h
        act1_h[step, HIDDEN:] = ones
        act1_l[step] = a1l
        z2 = dot(second_tk[...], jnp.concatenate([a1h, a1h, a1l], axis=0))
        a2h, a2l = split(jnp.maximum(z2 + second_b[...], 0.0))
        act2_h[step] = a2h
        act2_l[step] = a2l
        both = dot(last_thl[...], a2h)
        raw = both[:OUT_ROWS] + (both[OUT_ROWS:] + dot(last_thl[:OUT_ROWS], a2l)) + last_b[...]
        sc = sigmoid(raw[:CHANNELS])
        colors[step] = sc
        t = raw[CHANNELS : CHANNELS + 1]
        density = jnp.maximum(t, 0.0) + jnp.log1p(jnp.exp(-jnp.abs(t)))
        slope = sigmoid(t)
        image = misfit_ref[...]
        for g in range(TOGETHER):
            d = region(step, g)
            passed = jnp.exp(-cum)
            before = jnp.ones_like(cum)
            total = jnp.zeros_like(cum)
            rows[step, g, 9:10, :] = passed
            for s in range(SAMPLES):
                length = rays_ref[d, SAMPLES * FEAT + s : SAMPLES * FEAT + s + 1, :]
                optical = part(density, g, s) * length
                weight = before * (1.0 - jnp.exp(-optical))
                total = total + optical
                before = jnp.exp(-total)
                image = image + (passed * weight) * part(sc, g, s)
                rows[step, g, s : s + 1, :] = weight
                rows[step, g, SAMPLES + s : SAMPLES + s + 1, :] = before
                rows[step, g, 2 * SAMPLES + s : 2 * SAMPLES + s + 1, :] = part(slope, g, s) * length
            cum = cum + total
        misfit_ref[...] = image
        return cum

    steps = regions // TOGETHER
    lax.fori_loop(0, steps, forward, jnp.zeros((1, segment), f32), unroll=UNROLL)
    pixels = misfit_ref[...]
    misfit_ref[...] = pixels - target_ref[...]
    if first:
        pixels_ref[...] = pixels
    else:
        pixels_ref[...] = jnp.concatenate([pixels_in[...], pixels], axis=1)

    def backward(turn, behind):
        step = steps - 1 - turn
        misfit = misfit_ref[...]
        slopes = [None] * len(pieces)
        parts = [None] * len(pieces)
        for g in reversed(range(TOGETHER)):
            passed = rows[step, g, 9:10, :]
            later = -behind
            for s in reversed(range(SAMPLES)):
                i = g * SAMPLES + s
                weight = rows[step, g, s : s + 1, :]
                after = rows[step, g, SAMPLES + s : SAMPLES + s + 1, :]
                sc = colors[step, :, i * segment : (i + 1) * segment]
                product = misfit * sc
                value = passed * jnp.sum(product, axis=0, keepdims=True)
                parts[i] = (passed * weight) * (product - product * sc)
                slopes[i] = (value * after + later) * rows[step, g, 2 * SAMPLES + s : 2 * SAMPLES + s + 1, :]
                later = later - weight * value
            behind = -later
        d3 = jnp.concatenate(
            [
                jnp.concatenate(parts, axis=1),
                jnp.concatenate(slopes, axis=1),
                jnp.zeros((OUT_ROWS - OUT, columns), f32),
            ],
            axis=0,
        )
        bias3[...] += sum(part(d3, g, s) for g, s in pieces)
        d3h, d3l = split(d3)
        a2h = act2_h[step]
        d2 = dot(last_k[...], jnp.concatenate([d3h, d3l, d3h], axis=0))
        d2 = jnp.where(a2h > 0, d2, 0.0)
        d2h, d2l = split(d2)
        both = dot_columns(jnp.concatenate([d3h, d3l], axis=0), a2h)
        grad3[...] += both[:OUT_ROWS] + (both[OUT_ROWS:] + dot_columns(d3h, act2_l[step]))
        a1h = act1_h[step]
        d1 = dot(second_k[...], jnp.concatenate([d2h, d2h, d2l], axis=0))
        d1 = jnp.where(a1h[:HIDDEN] > 0, d1, 0.0)
        grad2[...] += dot_columns(a1h, d2h) + dot_columns(a1h, d2l)
        grad2[:HIDDEN] += dot_columns(act1_l[step], d2h)
        d1h, d1l = split(d1)
        xh, xl = inputs(step)
        both = dot_columns(jnp.concatenate([xh, ones, xl], axis=0), d1h)
        other = dot_columns(jnp.concatenate([xh, ones], axis=0), d1l)
        grad1[...] += both[: FEAT + ONES] + other
        grad1[:FEAT] += both[FEAT + ONES :]
        return behind

    lax.fori_loop(0, steps, backward, jnp.zeros((1, segment), f32), unroll=UNROLL)
    if not final:
        return

    half = HIDDEN // 2
    third = lax.dot_general(
        jnp.ones((8, segment), f32),
        jnp.concatenate([bias3[...], jnp.zeros((half - OUT_ROWS, segment), f32)], axis=0),
        (((1,), (1,)), ((), ())),
        precision=lax.Precision.HIGHEST,
        preferred_element_type=f32,
    )
    for side in range(2):
        lanes = slice(side * half, (side + 1) * half)
        grads_ref[side * 256 : side * 256 + 256] = grad2[:HIDDEN, lanes]
        grads_ref[512 + side * 32 : 544 + side * 32] = grad1[:FEAT, lanes]
        grads_ref[576 + side * 80 : 656 + side * 80] = grad3[:, lanes]
        misc = [grad1[FEAT : FEAT + 1, lanes], grad2[HIDDEN : HIDDEN + 1, lanes], third[0:1]]
        grads_ref[736 + side * 8 : 744 + side * 8] = jnp.concatenate(misc + [jnp.zeros((5, half), f32)], axis=0)
    grads_ref[752:] = jnp.zeros((PACKED - 752, half), f32)


def finish_kernel(sums_ref, first_ref, first_b_ref, second_ref, second_b_ref, last_t_ref, last_b_ref):
    def scale(parts, count):
        squares = sum(jnp.sum(part * part, keepdims=True) for part in parts)
        return 1.0 / jnp.sqrt(squares / count + epsilon)

    def both(start, rows, stride):
        return [sums_ref[start : start + rows, :], sums_ref[start + stride : start + stride + rows, :]]

    parts = both(0, 256, 256)
    second_ref[...] = jnp.concatenate(parts, axis=1) * scale(parts, HIDDEN * HIDDEN)
    parts = both(512, 32, 32)
    first_ref[...] = jnp.concatenate(parts, axis=1) * scale(parts, FEAT * HIDDEN)
    parts = both(576, 80, 80)
    last_t_ref[...] = jnp.concatenate(parts, axis=1)[:OUT] * scale(parts, HIDDEN * OUT)
    parts = both(736, 1, 8)
    first_b_ref[...] = jnp.concatenate(parts, axis=1) * scale(parts, HIDDEN)
    parts = both(737, 1, 8)
    second_b_ref[...] = jnp.concatenate(parts, axis=1) * scale(parts, HIDDEN)
    part = sums_ref[738:739, :]
    last_b_ref[...] = (part * scale([part], OUT))[:, :OUT]


vmem = pl.BlockSpec(memory_space=pltpu.VMEM)


def shaped(*shape, dtype=f32):
    return jax.ShapeDtypeStruct(shape, dtype)


def prepare_weights(first_weight, first_bias, second_weight, second_bias, last_weight, last_bias):
    return pl.pallas_call(
        weights_kernel,
        in_specs=[vmem] * 6,
        out_specs=[vmem] * 7,
        out_shape=[
            shaped(HIDDEN, 3 * FEAT + ONES, dtype=bf16),
            shaped(HIDDEN, 3 * HIDDEN, dtype=bf16),
            shaped(HIDDEN, 3 * HIDDEN, dtype=bf16),
            shaped(HIDDEN, 1),
            shaped(HIDDEN, 3 * OUT_ROWS, dtype=bf16),
            shaped(2 * OUT_ROWS, HIDDEN, dtype=bf16),
            shaped(OUT_ROWS, 1),
        ],
    )(first_weight, first_bias[None], second_weight, second_bias[None], last_weight.T, last_bias[None])


def step(first, final, flip, rays, target, weights, carried):
    regions, _, segment = rays.shape
    columns = TOGETHER * SAMPLES * segment
    steps = regions // TOGETHER
    sums = [
        shaped(FEAT + ONES, HIDDEN),
        shaped(HIDDEN + ONES, HIDDEN),
        shaped(OUT_ROWS, HIDDEN),
        shaped(OUT_ROWS, segment),
    ]
    scratch = [
        pltpu.VMEM((steps, HIDDEN + ONES, columns), bf16),
        pltpu.VMEM((steps, HIDDEN, columns), bf16),
        pltpu.VMEM((steps, HIDDEN, columns), bf16),
        pltpu.VMEM((steps, HIDDEN, columns), bf16),
        pltpu.VMEM((steps, CHANNELS, columns), f32),
        pltpu.VMEM((steps, TOGETHER, 16, segment), f32),
        pltpu.VMEM((CHANNELS, segment), f32),
    ]
    width = segment if first else 2 * segment
    if final:
        out_shape = [shaped(CHANNELS, width), shaped(PACKED, 128)]
        scratch = [pltpu.VMEM(s.shape, f32) for s in sums] + scratch
    else:
        out_shape = [shaped(CHANNELS, width)] + sums
    return pl.pallas_call(
        functools.partial(step_kernel, first, final),
        in_specs=[pl.BlockSpec(memory_space=pltpu.SMEM)] + [vmem] * (2 + len(weights) + len(carried)),
        out_specs=[vmem] * len(out_shape),
        out_shape=out_shape,
        scratch_shapes=scratch,
        compiler_params=pltpu.CompilerParams(vmem_limit_bytes=44 * 2**20),
        cost_estimate=pl.CostEstimate(
            flops=2 * 17 * 65536 * steps * columns, bytes_accessed=4 * 2**20, transcendentals=0
        ),
    )(flip, rays, target, *weights, *carried)


def local(
    features,
    spacing,
    counts,
    depth_rank,
    target,
    first_weight,
    first_bias,
    second_weight,
    second_bias,
    last_weight,
    last_bias,
):
    regions = lax.axis_size("depth")
    devices = regions * lax.axis_size("view")
    rays = features.shape[-1]
    lanes = rays // regions // PARTS
    flip = jnp.bitwise_xor(depth_rank[0, 0], lax.axis_index("depth")).reshape(1)

    sent = pl.pallas_call(
        send_kernel,
        in_specs=[vmem] * 3,
        out_specs=[vmem] * PARTS,
        out_shape=[shaped(regions, HEIGHT, lanes)] * PARTS,
    )(
        features[0, 0].transpose(1, 0, 2).reshape(SAMPLES * FEAT, rays),
        spacing[0, 0].reshape(SAMPLES, rays // 128, 128),
        counts[0, 0].reshape(rays // 128, 128),
    )
    got = [lax.all_to_all(part, "depth", 0, 0) for part in sent]
    weights = prepare_weights(first_weight, first_bias, second_weight, second_bias, last_weight, last_bias)
    carried = []
    for i in range(PARTS):
        goal = target[0, :, i * lanes : (i + 1) * lanes]
        carried = step(i == 0, i == PARTS - 1, flip, got[i], goal, weights, carried)
    pixels, grads = carried

    axes = ("view", "depth")
    shares = lax.all_to_all(grads.reshape(devices, PACKED // devices, 128), axes, 0, 0)
    share = jnp.sum(shares, axis=0)
    sums = lax.all_to_all(jnp.broadcast_to(share[None], shares.shape), axes, 0, 0)
    first_u, first_s, second_u, second_s, last_u, last_s = pl.pallas_call(
        finish_kernel,
        in_specs=[vmem],
        out_specs=[vmem] * 6,
        out_shape=[
            shaped(FEAT, HIDDEN),
            shaped(1, HIDDEN),
            shaped(HIDDEN, HIDDEN),
            shaped(1, HIDDEN),
            shaped(OUT, HIDDEN),
            shaped(1, OUT),
        ],
    )(sums.reshape(PACKED, 128))
    return (pixels[None], first_u, first_s[0], second_u, second_s[0], last_u.T, last_s[0])


def solution(mesh):
    return jax.shard_map(
        local,
        mesh=mesh,
        in_specs=(
            P("view", "depth", None, None, None),
            P("view", "depth", None, None),
            P("view", "depth", None),
            P("view", "depth"),
            P("view", None, "depth"),
            P(),
            P(),
            P(),
            P(),
            P(),
            P(),
        ),
        out_specs=(P("view", None, "depth"), P(), P(), P(), P(), P(), P()),
        check_vma=False,
    )
```

```python
import functools

import jax
import jax.numpy as jnp
from jax import lax
from jax.experimental import pallas as pl
from jax.experimental.pallas import tpu as pltpu
from jax.sharding import Mesh
from jax.sharding import PartitionSpec as P

epsilon = 1e-05
f32 = jnp.float32
bf16 = jnp.bfloat16
FEAT, HIDDEN, CHANNELS, SAMPLES = 32, 256, 64, 3
OUT = CHANNELS + 1
OUT_ROWS = 80
ONES = 16
HEIGHT = 104
PARTS = 2
TOGETHER = 4
UNROLL = 1
PACKED = 512


def split(value):
    high = value.astype(bf16)
    return high, (value - high.astype(f32)).astype(bf16)


def dot(left, right):
    return lax.dot_general(left, right, (((1,), (0,)), ((), ())), preferred_element_type=f32)


def dot_columns(left, right):
    return lax.dot_general(left, right, (((1,), (1,)), ((), ())), preferred_element_type=f32)


def sigmoid(value):
    return 0.5 * jnp.tanh(0.5 * value) + 0.5


def send_kernel(parts, i, features_ref, spacing_ref, counts_ref, sent_ref, lengths_ref, copies, small):
    regions, _, lanes = sent_ref.shape
    wide = lanes // 128
    started = []
    for j in range(regions):
        start = (j * parts + i) * lanes
        copy = pltpu.make_async_copy(
            features_ref.at[:, start : start + lanes], sent_ref.at[j, : SAMPLES * FEAT, :], copies.at[j]
        )
        copy.start()
        started.append(copy)
    lengths = [jnp.where(counts_ref[...] > s, spacing_ref[s], 0.0) for s in range(SAMPLES)]
    for j in range(regions):
        row = (j * parts + i) * wide
        for k in range(wide):
            lengths_ref[j, :, k * 128 : (k + 1) * 128] = jnp.concatenate(
                [v[row + k : row + k + 1] for v in lengths]
                + [jnp.zeros((HEIGHT - SAMPLES * FEAT - SAMPLES, 128), f32)],
                axis=0,
            )
    copy = pltpu.make_async_copy(lengths_ref, sent_ref.at[:, SAMPLES * FEAT :, :], small)
    copy.start()
    for done in started + [copy]:
        done.wait()


def weights_kernel(
    first_ref,
    first_bias_ref,
    second_ref,
    second_bias_ref,
    last_t_ref,
    last_bias_ref,
    first_k,
    second_k,
    second_tk,
    second_b,
    last_k,
    last_thl,
    last_b,
):
    def column(row, size):
        return jnp.transpose(jnp.broadcast_to(row, (8, size)))[:, 0:1]

    high, low = split(jnp.transpose(first_ref[...]))
    bias = column(first_bias_ref[...], HIDDEN)
    bias_h = bias.astype(bf16)
    rest = bias - bias_h.astype(f32)
    bias_m = rest.astype(bf16)
    bias_l = (rest - bias_m.astype(f32)).astype(bf16)
    pad = jnp.zeros((HIDDEN, ONES - 3), bf16)
    first_k[...] = jnp.concatenate([high, high, low, bias_h, bias_m, bias_l, pad], axis=1)
    high, low = split(second_ref[...])
    second_k[...] = jnp.concatenate([high, low, high], axis=1)
    high, low = split(jnp.transpose(second_ref[...]))
    second_tk[...] = jnp.concatenate([high, low, high], axis=1)
    second_b[...] = column(second_bias_ref[...], HIDDEN)
    last_t = jnp.concatenate([last_t_ref[...], jnp.zeros((128 - OUT, HIDDEN), f32)], axis=0)
    high, low = split(last_t[:OUT_ROWS])
    last_thl[...] = jnp.concatenate([high, low], axis=0)
    high, low = split(jnp.transpose(last_t)[:, :OUT_ROWS])
    last_k[...] = jnp.concatenate([high, high, low], axis=1)
    row = jnp.concatenate([last_bias_ref[...], jnp.zeros((1, 128 - OUT), f32)], axis=1)
    last_b[...] = column(row, 128)[:OUT_ROWS]


def step_kernel(first, final, place_ref, rays_ref, target_ref, *refs):
    first_k, second_k, second_tk, second_b, last_k, last_thl, last_b = refs[:7]
    refs = refs[7:]
    if not first:
        pixels_in, grad1_in, grad2_in, grad3_in, bias3_in = refs[:5]
        refs = refs[5:]
    if final:
        pixels_ref, keep_ref, send_ref = refs[:3]
        grad1, grad2, grad3, bias3 = refs[3:7]
        refs = refs[7:]
    else:
        pixels_ref, grad1, grad2, grad3, bias3 = refs[:5]
        refs = refs[5:]
    act1_h, act1_l, act2_h, act2_l, colors, rows, misfit_ref = refs
    regions, _, segment = rays_ref.shape
    flip = place_ref[0]
    pieces = [(g, s) for g in range(TOGETHER) for s in range(SAMPLES)]
    columns = len(pieces) * segment

    if first:
        grad1[...] = jnp.zeros_like(grad1)
        grad2[...] = jnp.zeros_like(grad2)
        grad3[...] = jnp.zeros_like(grad3)
        bias3[...] = jnp.zeros_like(bias3)
    else:
        grad1[...] = grad1_in[...]
        grad2[...] = grad2_in[...]
        grad3[...] = grad3_in[...]
        bias3[...] = bias3_in[...]
    misfit_ref[...] = jnp.zeros_like(misfit_ref)
    ones = jnp.ones((ONES, columns), bf16)

    def part(value, g, s):
        start = (g * SAMPLES + s) * segment
        return value[:, start : start + segment]

    def region(step, g):
        return jnp.bitwise_xor(step * TOGETHER + g, flip)

    def inputs(step):
        x = [rays_ref[region(step, g), s * FEAT : (s + 1) * FEAT, :] for g, s in pieces]
        return split(jnp.concatenate(x, axis=1))

    def forward(step, cum):
        xh, xl = inputs(step)
        a1 = jnp.maximum(dot(first_k[...], jnp.concatenate([xh, xl, xh, ones], axis=0)), 0.0)
        a1h, a1l = split(a1)
        act1_h[step, :HIDDEN] = a1h
        act1_h[step, HIDDEN:] = ones
        act1_l[step] = a1l
        z2 = dot(second_tk[...], jnp.concatenate([a1h, a1h, a1l], axis=0))
        a2h, a2l = split(jnp.maximum(z2 + second_b[...], 0.0))
        act2_h[step] = a2h
        act2_l[step] = a2l
        both = dot(last_thl[...], a2h)
        raw = both[:OUT_ROWS] + (both[OUT_ROWS:] + dot(last_thl[:OUT_ROWS], a2l)) + last_b[...]
        sc = sigmoid(raw[:CHANNELS])
        colors[step] = sc
        t = raw[CHANNELS : CHANNELS + 1]
        density = jnp.maximum(t, 0.0) + jnp.log1p(jnp.exp(-jnp.abs(t)))
        slope = sigmoid(t)
        image = misfit_ref[...]
        for g in range(TOGETHER):
            d = region(step, g)
            passed = jnp.exp(-cum)
            before = jnp.ones_like(cum)
            total = jnp.zeros_like(cum)
            rows[step, g, 9:10, :] = passed
            for s in range(SAMPLES):
                length = rays_ref[d, SAMPLES * FEAT + s : SAMPLES * FEAT + s + 1, :]
                optical = part(density, g, s) * length
                weight = before * (1.0 - jnp.exp(-optical))
                total = total + optical
                before = jnp.exp(-total)
                image = image + (passed * weight) * part(sc, g, s)
                rows[step, g, s : s + 1, :] = weight
                rows[step, g, SAMPLES + s : SAMPLES + s + 1, :] = before
                rows[step, g, 2 * SAMPLES + s : 2 * SAMPLES + s + 1, :] = part(slope, g, s) * length
            cum = cum + total
        misfit_ref[...] = image
        return cum

    steps = regions // TOGETHER
    lax.fori_loop(0, steps, forward, jnp.zeros((1, segment), f32), unroll=UNROLL)
    pixels = misfit_ref[...]
    misfit_ref[...] = pixels - target_ref[...]
    if first:
        pixels_ref[...] = pixels
    else:
        pixels_ref[...] = jnp.concatenate([pixels_in[...], pixels], axis=1)

    def backward(turn, behind):
        step = steps - 1 - turn
        misfit = misfit_ref[...]
        slopes = [None] * len(pieces)
        parts = [None] * len(pieces)
        for g in reversed(range(TOGETHER)):
            passed = rows[step, g, 9:10, :]
            later = -behind
            for s in reversed(range(SAMPLES)):
                i = g * SAMPLES + s
                weight = rows[step, g, s : s + 1, :]
                after = rows[step, g, SAMPLES + s : SAMPLES + s + 1, :]
                sc = colors[step, :, i * segment : (i + 1) * segment]
                product = misfit * sc
                value = passed * jnp.sum(product, axis=0, keepdims=True)
                parts[i] = (passed * weight) * (product - product * sc)
                slopes[i] = (value * after + later) * rows[step, g, 2 * SAMPLES + s : 2 * SAMPLES + s + 1, :]
                later = later - weight * value
            behind = -later
        d3 = jnp.concatenate(
            [
                jnp.concatenate(parts, axis=1),
                jnp.concatenate(slopes, axis=1),
                jnp.zeros((OUT_ROWS - OUT, columns), f32),
            ],
            axis=0,
        )
        bias3[...] += sum(part(d3, g, s) for g, s in pieces)
        d3h, d3l = split(d3)
        a2h = act2_h[step]
        d2 = dot(last_k[...], jnp.concatenate([d3h, d3l, d3h], axis=0))
        d2 = jnp.where(a2h > 0, d2, 0.0)
        d2h, d2l = split(d2)
        both = dot_columns(jnp.concatenate([d3h, d3l], axis=0), a2h)
        grad3[...] += both[:OUT_ROWS] + (both[OUT_ROWS:] + dot_columns(d3h, act2_l[step]))
        a1h = act1_h[step]
        d1 = dot(second_k[...], jnp.concatenate([d2h, d2h, d2l], axis=0))
        d1 = jnp.where(a1h[:HIDDEN] > 0, d1, 0.0)
        grad2[...] += dot_columns(a1h, d2h) + dot_columns(a1h, d2l)
        grad2[:HIDDEN] += dot_columns(act1_l[step], d2h)
        d1h, d1l = split(d1)
        xh, xl = inputs(step)
        both = dot_columns(jnp.concatenate([xh, ones, xl], axis=0), d1h)
        other = dot_columns(jnp.concatenate([xh, ones], axis=0), d1l)
        grad1[...] += both[: FEAT + ONES] + other
        grad1[:FEAT] += both[FEAT + ONES :]
        return behind

    lax.fori_loop(0, steps, backward, jnp.zeros((1, segment), f32), unroll=UNROLL)
    if not final:
        return

    half = HIDDEN // 2
    third = lax.dot_general(
        jnp.ones((8, segment), f32),
        jnp.concatenate([bias3[...], jnp.zeros((half - OUT_ROWS, segment), f32)], axis=0),
        (((1,), (1,)), ((), ())),
        precision=lax.Precision.HIGHEST,
        preferred_element_type=f32,
    )

    def pack(hidden_ref, others_ref):
        for side in range(2):
            lanes = slice(side * half, (side + 1) * half)
            hidden_ref[side * 256 : side * 256 + 256] = grad2[:HIDDEN, lanes]
            others_ref[side * 32 : 32 + side * 32] = grad1[:FEAT, lanes]
            others_ref[64 + side * 80 : 144 + side * 80] = grad3[:, lanes]
            misc = [grad1[FEAT : FEAT + 1, lanes], grad2[HIDDEN : HIDDEN + 1, lanes], third[0:1]]
            others_ref[224 + side * 8 : 232 + side * 8] = jnp.concatenate(misc + [jnp.zeros((5, half), f32)], axis=0)
        others_ref[240:] = jnp.zeros((PACKED - 240, half), f32)

    @pl.when(place_ref[1] == 0)
    def _():
        pack(keep_ref, send_ref)

    @pl.when(place_ref[1] == 1)
    def _():
        pack(send_ref, keep_ref)


def finish_kernel(place_ref, own_ref, other_ref, first_ref, first_b_ref, second_ref, second_b_ref, last_t_ref, last_b_ref):
    def scale(parts, count):
        squares = sum(jnp.sum(part * part, keepdims=True) for part in parts)
        return 1.0 / jnp.sqrt(squares / count + epsilon)

    def finish(hidden_ref, others_ref):
        def both(ref, start, rows, stride):
            return [ref[start : start + rows, :], ref[start + stride : start + stride + rows, :]]

        parts = both(hidden_ref, 0, 256, 256)
        second_ref[...] = jnp.concatenate(parts, axis=1) * scale(parts, HIDDEN * HIDDEN)
        parts = both(others_ref, 0, 32, 32)
        first_ref[...] = jnp.concatenate(parts, axis=1) * scale(parts, FEAT * HIDDEN)
        parts = both(others_ref, 64, 80, 80)
        last_t_ref[...] = jnp.concatenate(parts, axis=1)[:OUT] * scale(parts, HIDDEN * OUT)
        parts = both(others_ref, 224, 1, 8)
        first_b_ref[...] = jnp.concatenate(parts, axis=1) * scale(parts, HIDDEN)
        parts = both(others_ref, 225, 1, 8)
        second_b_ref[...] = jnp.concatenate(parts, axis=1) * scale(parts, HIDDEN)
        part = others_ref[226:227, :]
        last_b_ref[...] = (part * scale([part], OUT))[:, :OUT]

    @pl.when(place_ref[1] == 0)
    def _():
        finish(own_ref, other_ref)

    @pl.when(place_ref[1] == 1)
    def _():
        finish(other_ref, own_ref)


vmem = pl.BlockSpec(memory_space=pltpu.VMEM)


def shaped(*shape, dtype=f32):
    return jax.ShapeDtypeStruct(shape, dtype)


def prepare_weights(first_weight, first_bias, second_weight, second_bias, last_weight, last_bias):
    return pl.pallas_call(
        weights_kernel,
        in_specs=[vmem] * 6,
        out_specs=[vmem] * 7,
        out_shape=[
            shaped(HIDDEN, 3 * FEAT + ONES, dtype=bf16),
            shaped(HIDDEN, 3 * HIDDEN, dtype=bf16),
            shaped(HIDDEN, 3 * HIDDEN, dtype=bf16),
            shaped(HIDDEN, 1),
            shaped(HIDDEN, 3 * OUT_ROWS, dtype=bf16),
            shaped(2 * OUT_ROWS, HIDDEN, dtype=bf16),
            shaped(OUT_ROWS, 1),
        ],
        compiler_params=pltpu.CompilerParams(vmem_limit_bytes=8 * 2**20),
    )(first_weight, first_bias[None], second_weight, second_bias[None], last_weight.T, last_bias[None])


def step(first, final, place, rays, target, weights, carried):
    regions, _, segment = rays.shape
    columns = TOGETHER * SAMPLES * segment
    steps = regions // TOGETHER
    sums = [
        shaped(FEAT + ONES, HIDDEN),
        shaped(HIDDEN + ONES, HIDDEN),
        shaped(OUT_ROWS, HIDDEN),
        shaped(OUT_ROWS, segment),
    ]
    scratch = [
        pltpu.VMEM((steps, HIDDEN + ONES, columns), bf16),
        pltpu.VMEM((steps, HIDDEN, columns), bf16),
        pltpu.VMEM((steps, HIDDEN, columns), bf16),
        pltpu.VMEM((steps, HIDDEN, columns), bf16),
        pltpu.VMEM((steps, CHANNELS, columns), f32),
        pltpu.VMEM((steps, TOGETHER, 16, segment), f32),
        pltpu.VMEM((CHANNELS, segment), f32),
    ]
    width = segment if first else 2 * segment
    if final:
        out_shape = [shaped(CHANNELS, width), shaped(PACKED, 128), shaped(PACKED, 128)]
        scratch = [pltpu.VMEM(s.shape, f32) for s in sums] + scratch
    else:
        out_shape = [shaped(CHANNELS, width)] + sums
    return pl.pallas_call(
        functools.partial(step_kernel, first, final),
        in_specs=[pl.BlockSpec(memory_space=pltpu.SMEM)] + [vmem] * (2 + len(weights) + len(carried)),
        out_specs=[vmem] * len(out_shape),
        out_shape=out_shape,
        scratch_shapes=scratch,
        compiler_params=pltpu.CompilerParams(vmem_limit_bytes=44 * 2**20),
        cost_estimate=pl.CostEstimate(
            flops=2 * 17 * 65536 * steps * columns, bytes_accessed=2**20, transcendentals=0
        ),
    )(place, rays, target, *weights, *carried)


def local(
    features,
    spacing,
    counts,
    depth_rank,
    target,
    first_weight,
    first_bias,
    second_weight,
    second_bias,
    last_weight,
    last_bias,
):
    regions = lax.axis_size("depth")
    chips = regions * lax.axis_size("chip")
    rays = features.shape[-1]
    lanes = rays // regions // PARTS
    place = jnp.stack([jnp.bitwise_xor(depth_rank[0, 0], lax.axis_index("depth")), lax.axis_index("core")])

    got = []
    for i in range(PARTS):
        sent = pl.pallas_call(
            functools.partial(send_kernel, PARTS, i),
            in_specs=[pl.BlockSpec(memory_space=pl.ANY), vmem, vmem],
            out_specs=pl.BlockSpec(memory_space=pl.ANY),
            out_shape=shaped(regions, HEIGHT, lanes),
            scratch_shapes=[
                pltpu.VMEM((regions, HEIGHT - SAMPLES * FEAT, lanes), f32),
                pltpu.SemaphoreType.DMA((regions,)),
                pltpu.SemaphoreType.DMA,
            ],
            cost_estimate=pl.CostEstimate(flops=0, bytes_accessed=2**20, transcendentals=0),
        )(
            features[0, 0].transpose(1, 0, 2).reshape(SAMPLES * FEAT, rays),
            spacing[0, 0].reshape(SAMPLES, rays // 128, 128),
            counts[0, 0].reshape(rays // 128, 128),
        )
        got.append(lax.all_to_all(sent, "depth", 0, 0))
    weights = prepare_weights(first_weight, first_bias, second_weight, second_bias, last_weight, last_bias)
    carried = []
    for i in range(PARTS):
        goal = target[0, :, i * lanes : (i + 1) * lanes]
        carried = step(i == 0, i == PARTS - 1, place, got[i], goal, weights, carried)
    pixels, keep, send = carried

    swap = [(0, 1), (1, 0)]
    axes = ("chip", "depth")
    half = keep + lax.ppermute(send, "core", swap)
    shares = lax.all_to_all(half.reshape(chips, PACKED // chips, 128), axes, 0, 0)
    share = jnp.sum(shares, axis=0)
    own = lax.all_to_all(jnp.broadcast_to(share[None], shares.shape), axes, 0, 0).reshape(PACKED, 128)
    other = lax.ppermute(own, "core", swap)
    first_u, first_s, second_u, second_s, last_u, last_s = pl.pallas_call(
        finish_kernel,
        in_specs=[pl.BlockSpec(memory_space=pltpu.SMEM), vmem, vmem],
        out_specs=[vmem] * 6,
        out_shape=[
            shaped(FEAT, HIDDEN),
            shaped(1, HIDDEN),
            shaped(HIDDEN, HIDDEN),
            shaped(1, HIDDEN),
            shaped(OUT, HIDDEN),
            shaped(1, OUT),
        ],
        compiler_params=pltpu.CompilerParams(vmem_limit_bytes=8 * 2**20),
    )(place, own, other)
    return (pixels[None], first_u, first_s[0], second_u, second_s[0], last_u.T, last_s[0])


def solution(mesh):
    views, regions = mesh.devices.shape
    cores = 2
    mesh = Mesh(mesh.devices.reshape(views // cores, cores, regions), ("chip", "core", "depth"))
    view = ("chip", "core")
    return jax.shard_map(
        local,
        mesh=mesh,
        in_specs=(
            P(view, "depth", None, None, None),
            P(view, "depth", None, None),
            P(view, "depth", None),
            P(view, "depth"),
            P(view, None, "depth"),
            P(),
            P(),
            P(),
            P(),
            P(),
            P(),
        ),
        out_specs=(P(view, None, "depth"), P(), P(), P(), P(), P(), P()),
        check_vma=False,
    )
```

```python
import functools

import jax
import jax.numpy as jnp
from jax import lax
from jax.experimental import pallas as pl
from jax.experimental.pallas import tpu as pltpu
from jax.sharding import Mesh
from jax.sharding import PartitionSpec as P

epsilon = 1e-05
f32 = jnp.float32
bf16 = jnp.bfloat16
FEAT, HIDDEN, CHANNELS, SAMPLES = 32, 256, 64, 3
OUT = CHANNELS + 1
OUT_ROWS = 80
ONES = 16
HEIGHT = 104
PARTS = 2
TOGETHER = 4
UNROLL = 1
PACKED = 512


def split(value):
    high = value.astype(bf16)
    return high, (value - high.astype(f32)).astype(bf16)


def dot(left, right):
    return lax.dot_general(left, right, (((1,), (0,)), ((), ())), preferred_element_type=f32)


def dot_columns(left, right):
    return lax.dot_general(left, right, (((1,), (1,)), ((), ())), preferred_element_type=f32)


def sigmoid(value):
    return 0.5 * jnp.tanh(0.5 * value) + 0.5


def send_kernel(parts, i, features_ref, spacing_ref, counts_ref, sent_ref, copies):
    regions, _, lanes = sent_ref.shape
    wide = lanes // 128
    started = []
    for j in range(regions):
        start = (j * parts + i) * lanes
        copy = pltpu.make_async_copy(
            features_ref.at[:, start : start + lanes], sent_ref.at[j, : SAMPLES * FEAT, :], copies.at[j]
        )
        copy.start()
        started.append(copy)
    lengths = [jnp.where(counts_ref[...] > s, spacing_ref[s], 0.0) for s in range(SAMPLES)]
    for j in range(regions):
        row = (j * parts + i) * wide
        for k in range(wide):
            sent_ref[j, SAMPLES * FEAT :, k * 128 : (k + 1) * 128] = jnp.concatenate(
                [v[row + k : row + k + 1] for v in lengths]
                + [jnp.zeros((HEIGHT - SAMPLES * FEAT - SAMPLES, 128), f32)],
                axis=0,
            )
    for copy in started:
        copy.wait()


def weights_kernel(
    first_ref,
    first_bias_ref,
    second_ref,
    second_bias_ref,
    last_t_ref,
    last_bias_ref,
    first_k,
    second_k,
    second_tk,
    second_b,
    last_k,
    last_thl,
    last_b,
):
    def column(row, size):
        return jnp.transpose(jnp.broadcast_to(row, (8, size)))[:, 0:1]

    high, low = split(jnp.transpose(first_ref[...]))
    bias = column(first_bias_ref[...], HIDDEN)
    bias_h = bias.astype(bf16)
    rest = bias - bias_h.astype(f32)
    bias_m = rest.astype(bf16)
    bias_l = (rest - bias_m.astype(f32)).astype(bf16)
    pad = jnp.zeros((HIDDEN, ONES - 3), bf16)
    first_k[...] = jnp.concatenate([high, high, low, bias_h, bias_m, bias_l, pad], axis=1)
    high, low = split(second_ref[...])
    second_k[...] = jnp.concatenate([high, low, high], axis=1)
    high, low = split(jnp.transpose(second_ref[...]))
    second_tk[...] = jnp.concatenate([high, low, high], axis=1)
    second_b[...] = column(second_bias_ref[...], HIDDEN)
    last_t = jnp.concatenate([last_t_ref[...], jnp.zeros((128 - OUT, HIDDEN), f32)], axis=0)
    high, low = split(last_t[:OUT_ROWS])
    last_thl[...] = jnp.concatenate([high, low], axis=0)
    high, low = split(jnp.transpose(last_t)[:, :OUT_ROWS])
    last_k[...] = jnp.concatenate([high, high, low], axis=1)
    row = jnp.concatenate([last_bias_ref[...], jnp.zeros((1, 128 - OUT), f32)], axis=1)
    last_b[...] = column(row, 128)[:OUT_ROWS]


def step_kernel(first, final, place_ref, rays_ref, target_ref, *refs):
    first_k, second_k, second_tk, second_b, last_k, last_thl, last_b = refs[:7]
    refs = refs[7:]
    if not first:
        pixels_in, grad1_in, grad2_in, grad3_in, bias3_in = refs[:5]
        refs = refs[5:]
    if final:
        pixels_ref, keep_ref, send_ref = refs[:3]
        grad1, grad2, grad3, bias3 = refs[3:7]
        refs = refs[7:]
    else:
        pixels_ref, grad1, grad2, grad3, bias3 = refs[:5]
        refs = refs[5:]
    act1_h, act1_l, act2_h, act2_l, colors, rows, misfit_ref = refs
    regions, _, segment = rays_ref.shape
    flip = place_ref[0]
    pieces = [(g, s) for g in range(TOGETHER) for s in range(SAMPLES)]
    columns = len(pieces) * segment

    if first:
        grad1[...] = jnp.zeros_like(grad1)
        grad2[...] = jnp.zeros_like(grad2)
        grad3[...] = jnp.zeros_like(grad3)
        bias3[...] = jnp.zeros_like(bias3)
    else:
        grad1[...] = grad1_in[...]
        grad2[...] = grad2_in[...]
        grad3[...] = grad3_in[...]
        bias3[...] = bias3_in[...]
    misfit_ref[...] = jnp.zeros_like(misfit_ref)
    ones = jnp.ones((ONES, columns), bf16)

    def part(value, g, s):
        start = (g * SAMPLES + s) * segment
        return value[:, start : start + segment]

    def region(step, g):
        return jnp.bitwise_xor(step * TOGETHER + g, flip)

    def inputs(step):
        x = [rays_ref[region(step, g), s * FEAT : (s + 1) * FEAT, :] for g, s in pieces]
        return split(jnp.concatenate(x, axis=1))

    def forward(step, cum):
        xh, xl = inputs(step)
        a1 = jnp.maximum(dot(first_k[...], jnp.concatenate([xh, xl, xh, ones], axis=0)), 0.0)
        a1h, a1l = split(a1)
        act1_h[step, :HIDDEN] = a1h
        act1_h[step, HIDDEN:] = ones
        act1_l[step] = a1l
        z2 = dot(second_tk[...], jnp.concatenate([a1h, a1h, a1l], axis=0))
        a2h, a2l = split(jnp.maximum(z2 + second_b[...], 0.0))
        act2_h[step] = a2h
        act2_l[step] = a2l
        both = dot(last_thl[...], a2h)
        raw = both[:OUT_ROWS] + (both[OUT_ROWS:] + dot(last_thl[:OUT_ROWS], a2l)) + last_b[...]
        sc = sigmoid(raw[:CHANNELS])
        colors[step] = sc
        t = raw[CHANNELS : CHANNELS + 1]
        density = jnp.maximum(t, 0.0) + jnp.log1p(jnp.exp(-jnp.abs(t)))
        slope = sigmoid(t)
        image = misfit_ref[...]
        for g in range(TOGETHER):
            d = region(step, g)
            passed = jnp.exp(-cum)
            before = jnp.ones_like(cum)
            total = jnp.zeros_like(cum)
            rows[step, g, 9:10, :] = passed
            for s in range(SAMPLES):
                length = rays_ref[d, SAMPLES * FEAT + s : SAMPLES * FEAT + s + 1, :]
                optical = part(density, g, s) * length
                weight = before * (1.0 - jnp.exp(-optical))
                total = total + optical
                before = jnp.exp(-total)
                image = image + (passed * weight) * part(sc, g, s)
                rows[step, g, s : s + 1, :] = weight
                rows[step, g, SAMPLES + s : SAMPLES + s + 1, :] = before
                rows[step, g, 2 * SAMPLES + s : 2 * SAMPLES + s + 1, :] = part(slope, g, s) * length
            cum = cum + total
        misfit_ref[...] = image
        return cum

    steps = regions // TOGETHER
    lax.fori_loop(0, steps, forward, jnp.zeros((1, segment), f32), unroll=UNROLL)
    pixels = misfit_ref[...]
    misfit_ref[...] = pixels - target_ref[...]
    if first:
        pixels_ref[...] = pixels
    else:
        pixels_ref[...] = jnp.concatenate([pixels_in[...], pixels], axis=1)

    def backward(turn, behind):
        step = steps - 1 - turn
        misfit = misfit_ref[...]
        slopes = [None] * len(pieces)
        parts = [None] * len(pieces)
        for g in reversed(range(TOGETHER)):
            passed = rows[step, g, 9:10, :]
            later = -behind
            for s in reversed(range(SAMPLES)):
                i = g * SAMPLES + s
                weight = rows[step, g, s : s + 1, :]
                after = rows[step, g, SAMPLES + s : SAMPLES + s + 1, :]
                sc = colors[step, :, i * segment : (i + 1) * segment]
                product = misfit * sc
                value = passed * jnp.sum(product, axis=0, keepdims=True)
                parts[i] = (passed * weight) * (product - product * sc)
                slopes[i] = (value * after + later) * rows[step, g, 2 * SAMPLES + s : 2 * SAMPLES + s + 1, :]
                later = later - weight * value
            behind = -later
        d3 = jnp.concatenate(
            [
                jnp.concatenate(parts, axis=1),
                jnp.concatenate(slopes, axis=1),
                jnp.zeros((OUT_ROWS - OUT, columns), f32),
            ],
            axis=0,
        )
        bias3[...] += sum(part(d3, g, s) for g, s in pieces)
        d3h, d3l = split(d3)
        a2h = act2_h[step]
        d2 = dot(last_k[...], jnp.concatenate([d3h, d3l, d3h], axis=0))
        d2 = jnp.where(a2h > 0, d2, 0.0)
        d2h, d2l = split(d2)
        both = dot_columns(jnp.concatenate([d3h, d3l], axis=0), a2h)
        grad3[...] += both[:OUT_ROWS] + (both[OUT_ROWS:] + dot_columns(d3h, act2_l[step]))
        a1h = act1_h[step]
        d1 = dot(second_k[...], jnp.concatenate([d2h, d2h, d2l], axis=0))
        d1 = jnp.where(a1h[:HIDDEN] > 0, d1, 0.0)
        grad2[...] += dot_columns(a1h, d2h) + dot_columns(a1h, d2l)
        grad2[:HIDDEN] += dot_columns(act1_l[step], d2h)
        d1h, d1l = split(d1)
        xh, xl = inputs(step)
        both = dot_columns(jnp.concatenate([xh, ones, xl], axis=0), d1h)
        other = dot_columns(jnp.concatenate([xh, ones], axis=0), d1l)
        grad1[...] += both[: FEAT + ONES] + other
        grad1[:FEAT] += both[FEAT + ONES :]
        return behind

    lax.fori_loop(0, steps, backward, jnp.zeros((1, segment), f32), unroll=UNROLL)
    if not final:
        return

    half = HIDDEN // 2
    third = lax.dot_general(
        jnp.ones((8, segment), f32),
        jnp.concatenate([bias3[...], jnp.zeros((half - OUT_ROWS, segment), f32)], axis=0),
        (((1,), (1,)), ((), ())),
        precision=lax.Precision.HIGHEST,
        preferred_element_type=f32,
    )

    def pack(hidden_ref, others_ref):
        for side in range(2):
            lanes = slice(side * half, (side + 1) * half)
            hidden_ref[side * 256 : side * 256 + 256] = grad2[:HIDDEN, lanes]
            others_ref[side * 32 : 32 + side * 32] = grad1[:FEAT, lanes]
            others_ref[64 + side * 80 : 144 + side * 80] = grad3[:, lanes]
            misc = [grad1[FEAT : FEAT + 1, lanes], grad2[HIDDEN : HIDDEN + 1, lanes], third[0:1]]
            others_ref[224 + side * 8 : 232 + side * 8] = jnp.concatenate(misc + [jnp.zeros((5, half), f32)], axis=0)
        others_ref[240:] = jnp.zeros((PACKED - 240, half), f32)

    @pl.when(place_ref[1] == 0)
    def _():
        pack(keep_ref, send_ref)

    @pl.when(place_ref[1] == 1)
    def _():
        pack(send_ref, keep_ref)


def finish_kernel(place_ref, own_ref, other_ref, first_ref, first_b_ref, second_ref, second_b_ref, last_t_ref, last_b_ref):
    def scale(parts, count):
        squares = sum(jnp.sum(part * part, keepdims=True) for part in parts)
        return 1.0 / jnp.sqrt(squares / count + epsilon)

    def finish(hidden_ref, others_ref):
        def both(ref, start, rows, stride):
            return [ref[start : start + rows, :], ref[start + stride : start + stride + rows, :]]

        parts = both(hidden_ref, 0, 256, 256)
        second_ref[...] = jnp.concatenate(parts, axis=1) * scale(parts, HIDDEN * HIDDEN)
        parts = both(others_ref, 0, 32, 32)
        first_ref[...] = jnp.concatenate(parts, axis=1) * scale(parts, FEAT * HIDDEN)
        parts = both(others_ref, 64, 80, 80)
        last_t_ref[...] = jnp.concatenate(parts, axis=1)[:OUT] * scale(parts, HIDDEN * OUT)
        parts = both(others_ref, 224, 1, 8)
        first_b_ref[...] = jnp.concatenate(parts, axis=1) * scale(parts, HIDDEN)
        parts = both(others_ref, 225, 1, 8)
        second_b_ref[...] = jnp.concatenate(parts, axis=1) * scale(parts, HIDDEN)
        part = others_ref[226:227, :]
        last_b_ref[...] = (part * scale([part], OUT))[:, :OUT]

    @pl.when(place_ref[1] == 0)
    def _():
        finish(own_ref, other_ref)

    @pl.when(place_ref[1] == 1)
    def _():
        finish(other_ref, own_ref)


vmem = pl.BlockSpec(memory_space=pltpu.VMEM)


def shaped(*shape, dtype=f32):
    return jax.ShapeDtypeStruct(shape, dtype)


def prepare_weights(first_weight, first_bias, second_weight, second_bias, last_weight, last_bias):
    return pl.pallas_call(
        weights_kernel,
        in_specs=[vmem] * 6,
        out_specs=[vmem] * 7,
        out_shape=[
            shaped(HIDDEN, 3 * FEAT + ONES, dtype=bf16),
            shaped(HIDDEN, 3 * HIDDEN, dtype=bf16),
            shaped(HIDDEN, 3 * HIDDEN, dtype=bf16),
            shaped(HIDDEN, 1),
            shaped(HIDDEN, 3 * OUT_ROWS, dtype=bf16),
            shaped(2 * OUT_ROWS, HIDDEN, dtype=bf16),
            shaped(OUT_ROWS, 1),
        ],
        compiler_params=pltpu.CompilerParams(vmem_limit_bytes=8 * 2**20),
    )(first_weight, first_bias[None], second_weight, second_bias[None], last_weight.T, last_bias[None])


def step(first, final, place, rays, target, weights, carried):
    regions, _, segment = rays.shape
    columns = TOGETHER * SAMPLES * segment
    steps = regions // TOGETHER
    sums = [
        shaped(FEAT + ONES, HIDDEN),
        shaped(HIDDEN + ONES, HIDDEN),
        shaped(OUT_ROWS, HIDDEN),
        shaped(OUT_ROWS, segment),
    ]
    scratch = [
        pltpu.VMEM((steps, HIDDEN + ONES, columns), bf16),
        pltpu.VMEM((steps, HIDDEN, columns), bf16),
        pltpu.VMEM((steps, HIDDEN, columns), bf16),
        pltpu.VMEM((steps, HIDDEN, columns), bf16),
        pltpu.VMEM((steps, CHANNELS, columns), f32),
        pltpu.VMEM((steps, TOGETHER, 16, segment), f32),
        pltpu.VMEM((CHANNELS, segment), f32),
    ]
    width = segment if first else 2 * segment
    if final:
        out_shape = [shaped(CHANNELS, width), shaped(PACKED, 128), shaped(PACKED, 128)]
        scratch = [pltpu.VMEM(s.shape, f32) for s in sums] + scratch
    else:
        out_shape = [shaped(CHANNELS, width)] + sums
    return pl.pallas_call(
        functools.partial(step_kernel, first, final),
        in_specs=[pl.BlockSpec(memory_space=pltpu.SMEM)] + [vmem] * (2 + len(weights) + len(carried)),
        out_specs=[vmem] * len(out_shape),
        out_shape=out_shape,
        scratch_shapes=scratch,
        compiler_params=pltpu.CompilerParams(vmem_limit_bytes=44 * 2**20),
        cost_estimate=pl.CostEstimate(
            flops=2 * 17 * 65536 * steps * columns, bytes_accessed=2**20, transcendentals=0
        ),
    )(place, rays, target, *weights, *carried)


def local(
    features,
    spacing,
    counts,
    depth_rank,
    target,
    first_weight,
    first_bias,
    second_weight,
    second_bias,
    last_weight,
    last_bias,
):
    regions = lax.axis_size("depth")
    chips = regions * lax.axis_size("chip")
    rays = features.shape[-1]
    lanes = rays // regions // PARTS
    place = jnp.stack([jnp.bitwise_xor(depth_rank[0, 0], lax.axis_index("depth")), lax.axis_index("core")])

    got = []
    for i in range(PARTS):
        sent = pl.pallas_call(
            functools.partial(send_kernel, PARTS, i),
            in_specs=[pl.BlockSpec(memory_space=pl.ANY), vmem, vmem],
            out_specs=vmem,
            out_shape=shaped(regions, HEIGHT, lanes),
            scratch_shapes=[pltpu.SemaphoreType.DMA((regions,))],
            cost_estimate=pl.CostEstimate(flops=0, bytes_accessed=2**20, transcendentals=0),
        )(
            features[0, 0].transpose(1, 0, 2).reshape(SAMPLES * FEAT, rays),
            spacing[0, 0].reshape(SAMPLES, rays // 128, 128),
            counts[0, 0].reshape(rays // 128, 128),
        )
        got.append(lax.all_to_all(sent, "depth", 0, 0))
    weights = prepare_weights(first_weight, first_bias, second_weight, second_bias, last_weight, last_bias)
    carried = []
    for i in range(PARTS):
        goal = target[0, :, i * lanes : (i + 1) * lanes]
        carried = step(i == 0, i == PARTS - 1, place, got[i], goal, weights, carried)
    pixels, keep, send = carried

    swap = [(0, 1), (1, 0)]
    axes = ("chip", "depth")
    half = keep + lax.ppermute(send, "core", swap)
    shares = lax.all_to_all(half.reshape(chips, PACKED // chips, 128), axes, 0, 0)
    share = jnp.sum(shares, axis=0)
    own = lax.all_to_all(jnp.broadcast_to(share[None], shares.shape), axes, 0, 0).reshape(PACKED, 128)
    other = lax.ppermute(own, "core", swap)
    first_u, first_s, second_u, second_s, last_u, last_s = pl.pallas_call(
        finish_kernel,
        in_specs=[pl.BlockSpec(memory_space=pltpu.SMEM), vmem, vmem],
        out_specs=[vmem] * 6,
        out_shape=[
            shaped(FEAT, HIDDEN),
            shaped(1, HIDDEN),
            shaped(HIDDEN, HIDDEN),
            shaped(1, HIDDEN),
            shaped(OUT, HIDDEN),
            shaped(1, OUT),
        ],
        compiler_params=pltpu.CompilerParams(vmem_limit_bytes=8 * 2**20),
    )(place, own, other)
    return (pixels[None], first_u, first_s[0], second_u, second_s[0], last_u.T, last_s[0])


def solution(mesh):
    views, regions = mesh.devices.shape
    cores = 2
    mesh = Mesh(mesh.devices.reshape(views // cores, cores, regions), ("chip", "core", "depth"))
    view = ("chip", "core")
    return jax.shard_map(
        local,
        mesh=mesh,
        in_specs=(
            P(view, "depth", None, None, None),
            P(view, "depth", None, None),
            P(view, "depth", None),
            P(view, "depth"),
            P(view, None, "depth"),
            P(),
            P(),
            P(),
            P(),
            P(),
            P(),
        ),
        out_specs=(P(view, None, "depth"), P(), P(), P(), P(), P(), P()),
        check_vma=False,
    )
```

```python
import functools

import jax
import jax.numpy as jnp
from jax import lax
from jax.experimental import pallas as pl
from jax.experimental.pallas import tpu as pltpu
from jax.sharding import Mesh
from jax.sharding import PartitionSpec as P

epsilon = 1e-05
f32 = jnp.float32
bf16 = jnp.bfloat16
FEAT, HIDDEN, CHANNELS, SAMPLES = 32, 256, 64, 3
OUT = CHANNELS + 1
OUT_ROWS = 80
ONES = 16
HEIGHT = 104
PARTS = 2
TOGETHER = 4
UNROLL = 2
WIDTH = 512
PACKED = 512


def split(value):
    high = value.astype(bf16)
    return high, (value - high.astype(f32)).astype(bf16)


def dot(left, right):
    return lax.dot_general(left, right, (((1,), (0,)), ((), ())), preferred_element_type=f32)


def dot_columns(left, right):
    return lax.dot_general(left, right, (((1,), (1,)), ((), ())), preferred_element_type=f32)


def sigmoid(value):
    return 0.5 * jnp.tanh(0.5 * value) + 0.5


def send_kernel(parts, i, features_ref, spacing_ref, counts_ref, sent_ref):
    regions, _, lanes = sent_ref.shape
    wide = lanes // 128
    lengths = [jnp.where(counts_ref[...] > s, spacing_ref[s], 0.0) for s in range(SAMPLES)]
    for j in range(regions):
        start = (j * parts + i) * lanes
        sent_ref[j, : SAMPLES * FEAT, :] = features_ref[:, start : start + lanes]
        row = (j * parts + i) * wide
        for k in range(wide):
            sent_ref[j, SAMPLES * FEAT :, k * 128 : (k + 1) * 128] = jnp.concatenate(
                [v[row + k : row + k + 1] for v in lengths]
                + [jnp.zeros((HEIGHT - SAMPLES * FEAT - SAMPLES, 128), f32)],
                axis=0,
            )


def weights_kernel(
    first_ref,
    first_bias_ref,
    second_ref,
    second_bias_ref,
    last_t_ref,
    last_bias_ref,
    first_k,
    second_k,
    second_tk,
    second_b,
    last_k,
    last_thl,
    last_b,
):
    def column(row, size):
        return jnp.transpose(jnp.broadcast_to(row, (8, size)))[:, 0:1]

    high, low = split(jnp.transpose(first_ref[...]))
    bias = column(first_bias_ref[...], HIDDEN)
    bias_h = bias.astype(bf16)
    rest = bias - bias_h.astype(f32)
    bias_m = rest.astype(bf16)
    bias_l = (rest - bias_m.astype(f32)).astype(bf16)
    pad = jnp.zeros((HIDDEN, ONES - 3), bf16)
    first_k[...] = jnp.concatenate([high, high, low, bias_h, bias_m, bias_l, pad], axis=1)
    high, low = split(second_ref[...])
    second_k[...] = jnp.concatenate([high, low, high], axis=1)
    high, low = split(jnp.transpose(second_ref[...]))
    second_tk[...] = jnp.concatenate([high, low, high], axis=1)
    second_b[...] = column(second_bias_ref[...], HIDDEN)
    last_t = jnp.concatenate([last_t_ref[...], jnp.zeros((128 - OUT, HIDDEN), f32)], axis=0)
    high, low = split(last_t[:OUT_ROWS])
    last_thl[...] = jnp.concatenate([high, low], axis=0)
    high, low = split(jnp.transpose(last_t)[:, :OUT_ROWS])
    last_k[...] = jnp.concatenate([high, high, low], axis=1)
    row = jnp.concatenate([last_bias_ref[...], jnp.zeros((1, 128 - OUT), f32)], axis=1)
    last_b[...] = column(row, 128)[:OUT_ROWS]


def step_kernel(first, final, place_ref, rays_ref, target_ref, *refs):
    first_k, second_k, second_tk, second_b, last_k, last_thl, last_b = refs[:7]
    refs = refs[7:]
    if not first:
        pixels_in, grad1_in, grad2_in, grad3_in, bias3_in = refs[:5]
        refs = refs[5:]
    if final:
        pixels_ref, keep_ref, send_ref = refs[:3]
        grad1, grad2, grad3, bias3 = refs[3:7]
        refs = refs[7:]
    else:
        pixels_ref, grad1, grad2, grad3, bias3 = refs[:5]
        refs = refs[5:]
    act1_h, act1_l, act2_h, act2_l, colors, rows, misfit_ref, logit, d3_hl, d2_h, d2_l, d1_h, d1_l = refs
    regions, _, segment = rays_ref.shape
    flip = place_ref[0]
    pieces = [(g, s) for g in range(TOGETHER) for s in range(SAMPLES)]
    columns = len(pieces) * segment

    if first:
        grad1[...] = jnp.zeros_like(grad1)
        grad2[...] = jnp.zeros_like(grad2)
        grad3[...] = jnp.zeros_like(grad3)
        bias3[...] = jnp.zeros_like(bias3)
    else:
        grad1[...] = grad1_in[...]
        grad2[...] = grad2_in[...]
        grad3[...] = grad3_in[...]
        bias3[...] = bias3_in[...]
    misfit_ref[...] = jnp.zeros_like(misfit_ref)
    def part(value, g, s):
        start = (g * SAMPLES + s) * segment
        return value[:, start : start + segment]

    def region(step, g):
        return jnp.bitwise_xor(step * TOGETHER + g, flip)

    per = WIDTH // segment
    tiles = columns // WIDTH

    def inputs(step, tile):
        x = [
            rays_ref[region(step, g), s * FEAT : (s + 1) * FEAT, :]
            for g, s in pieces[tile * per : (tile + 1) * per]
        ]
        return split(jnp.concatenate(x, axis=1))

    def at(tile):
        return slice(tile * WIDTH, (tile + 1) * WIDTH)

    def forward(step, cum):
        ones = jnp.ones((ONES, WIDTH), bf16)

        def first_layer(tile):
            xh, xl = inputs(step, tile)
            a1 = jnp.maximum(dot(first_k[...], jnp.concatenate([xh, xl, xh, ones], axis=0)), 0.0)
            a1h, a1l = split(a1)
            act1_h[step, :HIDDEN, at(tile)] = a1h
            act1_h[step, HIDDEN:, at(tile)] = ones
            act1_l[step, :, at(tile)] = a1l

        def second_layer(tile):
            a1h = act1_h[step, :HIDDEN, at(tile)]
            z2 = dot(second_tk[...], jnp.concatenate([a1h, a1h, act1_l[step, :, at(tile)]], axis=0))
            a2h, a2l = split(jnp.maximum(z2 + second_b[...], 0.0))
            act2_h[step, :, at(tile)] = a2h
            act2_l[step, :, at(tile)] = a2l

        def last_layer(tile):
            both = dot(last_thl[...], act2_h[step, :, at(tile)])
            low = dot(last_thl[:OUT_ROWS], act2_l[step, :, at(tile)])
            raw = both[:OUT_ROWS] + (both[OUT_ROWS:] + low) + last_b[...]
            colors[step, :, at(tile)] = sigmoid(raw[:CHANNELS])
            logit[:, at(tile)] = raw[CHANNELS : CHANNELS + 8]

        for stage in (first_layer, second_layer, last_layer):
            for tile in range(tiles):
                stage(tile)
        t = logit[0:1]
        density = jnp.maximum(t, 0.0) + jnp.log1p(jnp.exp(-jnp.abs(t)))
        slope = sigmoid(t)
        image = misfit_ref[...]
        for g in range(TOGETHER):
            d = region(step, g)
            passed = jnp.exp(-cum)
            before = jnp.ones_like(cum)
            total = jnp.zeros_like(cum)
            rows[step, g, 9:10, :] = passed
            for s in range(SAMPLES):
                i = g * SAMPLES + s
                length = rays_ref[d, SAMPLES * FEAT + s : SAMPLES * FEAT + s + 1, :]
                optical = part(density, g, s) * length
                weight = before * (1.0 - jnp.exp(-optical))
                total = total + optical
                before = jnp.exp(-total)
                image = image + (passed * weight) * colors[step, :, i * segment : (i + 1) * segment]
                rows[step, g, s : s + 1, :] = weight
                rows[step, g, SAMPLES + s : SAMPLES + s + 1, :] = before
                rows[step, g, 2 * SAMPLES + s : 2 * SAMPLES + s + 1, :] = part(slope, g, s) * length
            cum = cum + total
        misfit_ref[...] = image
        return cum

    steps = regions // TOGETHER
    lax.fori_loop(0, steps, forward, jnp.zeros((1, segment), f32), unroll=UNROLL)
    pixels = misfit_ref[...]
    misfit_ref[...] = pixels - target_ref[...]
    if first:
        pixels_ref[...] = pixels
    else:
        pixels_ref[...] = jnp.concatenate([pixels_in[...], pixels], axis=1)

    def backward(turn, behind):
        step = steps - 1 - turn
        misfit = misfit_ref[...]
        slopes = [None] * len(pieces)
        parts = [None] * len(pieces)
        for g in reversed(range(TOGETHER)):
            passed = rows[step, g, 9:10, :]
            later = -behind
            for s in reversed(range(SAMPLES)):
                i = g * SAMPLES + s
                weight = rows[step, g, s : s + 1, :]
                after = rows[step, g, SAMPLES + s : SAMPLES + s + 1, :]
                sc = colors[step, :, i * segment : (i + 1) * segment]
                product = misfit * sc
                value = passed * jnp.sum(product, axis=0, keepdims=True)
                parts[i] = (passed * weight) * (product - product * sc)
                slopes[i] = (value * after + later) * rows[step, g, 2 * SAMPLES + s : 2 * SAMPLES + s + 1, :]
                later = later - weight * value
            behind = -later
        def output(tile):
            mine = slice(tile * per, (tile + 1) * per)
            d3 = jnp.concatenate(
                [
                    jnp.concatenate(parts[mine], axis=1),
                    jnp.concatenate(slopes[mine], axis=1),
                    jnp.zeros((OUT_ROWS - OUT, WIDTH), f32),
                ],
                axis=0,
            )
            high, low = split(d3)
            d3_hl[:OUT_ROWS, at(tile)] = high
            d3_hl[OUT_ROWS:, at(tile)] = low
            bias3[...] += sum(d3[:, i * segment : (i + 1) * segment] for i in range(per))

        def last_layer(tile):
            d3h = d3_hl[:OUT_ROWS, at(tile)]
            d2 = dot(last_k[...], jnp.concatenate([d3h, d3_hl[OUT_ROWS:, at(tile)], d3h], axis=0))
            high, low = split(d2)
            live = act2_h[step, :, at(tile)] > 0
            d2_h[:, at(tile)] = jnp.where(live, high, jnp.zeros_like(high))
            d2_l[:, at(tile)] = jnp.where(live, low, jnp.zeros_like(low))

        def second_layer(tile):
            high = d2_h[:, at(tile)]
            d1 = dot(second_k[...], jnp.concatenate([high, high, d2_l[:, at(tile)]], axis=0))
            high, low = split(d1)
            live = act1_h[step, :HIDDEN, at(tile)] > 0
            d1_h[:, at(tile)] = jnp.where(live, high, jnp.zeros_like(high))
            d1_l[:, at(tile)] = jnp.where(live, low, jnp.zeros_like(low))

        def sum_last():
            both = dot_columns(d3_hl[...], act2_h[step])
            low = dot_columns(d3_hl[:OUT_ROWS], act2_l[step])
            grad3[...] += both[:OUT_ROWS] + (both[OUT_ROWS:] + low)

        def sum_second():
            a1h = act1_h[step]
            grad2[...] += dot_columns(a1h, d2_h[...]) + dot_columns(a1h, d2_l[...])
            grad2[:HIDDEN] += dot_columns(act1_l[step], d2_h[...])

        def sum_first():
            x = [inputs(step, tile) for tile in range(tiles)]
            xh = jnp.concatenate([h for h, _ in x], axis=1)
            xl = jnp.concatenate([l for _, l in x], axis=1)
            ones = jnp.ones((ONES, columns), bf16)
            both = dot_columns(jnp.concatenate([xh, ones, xl], axis=0), d1_h[...])
            other = dot_columns(jnp.concatenate([xh, ones], axis=0), d1_l[...])
            grad1[...] += both[: FEAT + ONES] + other
            grad1[:FEAT] += both[FEAT + ONES :]

        for stage in (output, last_layer, second_layer):
            for tile in range(tiles):
                stage(tile)
        sum_last()
        sum_second()
        sum_first()
        return behind

    lax.fori_loop(0, steps, backward, jnp.zeros((1, segment), f32), unroll=UNROLL)
    if not final:
        return

    half = HIDDEN // 2
    third = lax.dot_general(
        jnp.ones((8, segment), f32),
        jnp.concatenate([bias3[...], jnp.zeros((half - OUT_ROWS, segment), f32)], axis=0),
        (((1,), (1,)), ((), ())),
        precision=lax.Precision.HIGHEST,
        preferred_element_type=f32,
    )

    def pack(hidden_ref, others_ref):
        for side in range(2):
            lanes = slice(side * half, (side + 1) * half)
            hidden_ref[side * 256 : side * 256 + 256] = grad2[:HIDDEN, lanes]
            others_ref[side * 32 : 32 + side * 32] = grad1[:FEAT, lanes]
            others_ref[64 + side * 80 : 144 + side * 80] = grad3[:, lanes]
            misc = [grad1[FEAT : FEAT + 1, lanes], grad2[HIDDEN : HIDDEN + 1, lanes], third[0:1]]
            others_ref[224 + side * 8 : 232 + side * 8] = jnp.concatenate(misc + [jnp.zeros((5, half), f32)], axis=0)
        others_ref[240:] = jnp.zeros((PACKED - 240, half), f32)

    @pl.when(place_ref[1] == 0)
    def _():
        pack(keep_ref, send_ref)

    @pl.when(place_ref[1] == 1)
    def _():
        pack(send_ref, keep_ref)


def finish_kernel(place_ref, own_ref, other_ref, first_ref, first_b_ref, second_ref, second_b_ref, last_t_ref, last_b_ref):
    def scale(parts, count):
        squares = sum(jnp.sum(part * part, keepdims=True) for part in parts)
        return 1.0 / jnp.sqrt(squares / count + epsilon)

    def finish(hidden_ref, others_ref):
        def both(ref, start, rows, stride):
            return [ref[start : start + rows, :], ref[start + stride : start + stride + rows, :]]

        parts = both(hidden_ref, 0, 256, 256)
        second_ref[...] = jnp.concatenate(parts, axis=1) * scale(parts, HIDDEN * HIDDEN)
        parts = both(others_ref, 0, 32, 32)
        first_ref[...] = jnp.concatenate(parts, axis=1) * scale(parts, FEAT * HIDDEN)
        parts = both(others_ref, 64, 80, 80)
        last_t_ref[...] = jnp.concatenate(parts, axis=1)[:OUT] * scale(parts, HIDDEN * OUT)
        parts = both(others_ref, 224, 1, 8)
        first_b_ref[...] = jnp.concatenate(parts, axis=1) * scale(parts, HIDDEN)
        parts = both(others_ref, 225, 1, 8)
        second_b_ref[...] = jnp.concatenate(parts, axis=1) * scale(parts, HIDDEN)
        part = others_ref[226:227, :]
        last_b_ref[...] = (part * scale([part], OUT))[:, :OUT]

    @pl.when(place_ref[1] == 0)
    def _():
        finish(own_ref, other_ref)

    @pl.when(place_ref[1] == 1)
    def _():
        finish(other_ref, own_ref)


vmem = pl.BlockSpec(memory_space=pltpu.VMEM)


def shaped(*shape, dtype=f32):
    return jax.ShapeDtypeStruct(shape, dtype)


def prepare_weights(first_weight, first_bias, second_weight, second_bias, last_weight, last_bias):
    return pl.pallas_call(
        weights_kernel,
        in_specs=[vmem] * 6,
        out_specs=[vmem] * 7,
        out_shape=[
            shaped(HIDDEN, 3 * FEAT + ONES, dtype=bf16),
            shaped(HIDDEN, 3 * HIDDEN, dtype=bf16),
            shaped(HIDDEN, 3 * HIDDEN, dtype=bf16),
            shaped(HIDDEN, 1),
            shaped(HIDDEN, 3 * OUT_ROWS, dtype=bf16),
            shaped(2 * OUT_ROWS, HIDDEN, dtype=bf16),
            shaped(OUT_ROWS, 1),
        ],
        compiler_params=pltpu.CompilerParams(vmem_limit_bytes=8 * 2**20),
    )(first_weight, first_bias[None], second_weight, second_bias[None], last_weight.T, last_bias[None])


def step(first, final, place, rays, target, weights, carried):
    regions, _, segment = rays.shape
    columns = TOGETHER * SAMPLES * segment
    steps = regions // TOGETHER
    sums = [
        shaped(FEAT + ONES, HIDDEN),
        shaped(HIDDEN + ONES, HIDDEN),
        shaped(OUT_ROWS, HIDDEN),
        shaped(OUT_ROWS, segment),
    ]
    scratch = [
        pltpu.VMEM((steps, HIDDEN + ONES, columns), bf16),
        pltpu.VMEM((steps, HIDDEN, columns), bf16),
        pltpu.VMEM((steps, HIDDEN, columns), bf16),
        pltpu.VMEM((steps, HIDDEN, columns), bf16),
        pltpu.VMEM((steps, CHANNELS, columns), f32),
        pltpu.VMEM((steps, TOGETHER, 16, segment), f32),
        pltpu.VMEM((CHANNELS, segment), f32),
        pltpu.VMEM((8, columns), f32),
        pltpu.VMEM((2 * OUT_ROWS, columns), bf16),
        pltpu.VMEM((HIDDEN, columns), bf16),
        pltpu.VMEM((HIDDEN, columns), bf16),
        pltpu.VMEM((HIDDEN, columns), bf16),
        pltpu.VMEM((HIDDEN, columns), bf16),
    ]
    width = segment if first else 2 * segment
    if final:
        out_shape = [shaped(CHANNELS, width), shaped(PACKED, 128), shaped(PACKED, 128)]
        scratch = [pltpu.VMEM(s.shape, f32) for s in sums] + scratch
    else:
        out_shape = [shaped(CHANNELS, width)] + sums
    return pl.pallas_call(
        functools.partial(step_kernel, first, final),
        in_specs=[pl.BlockSpec(memory_space=pltpu.SMEM)] + [vmem] * (2 + len(weights) + len(carried)),
        out_specs=[vmem] * len(out_shape),
        out_shape=out_shape,
        scratch_shapes=scratch,
        compiler_params=pltpu.CompilerParams(vmem_limit_bytes=44 * 2**20),
        cost_estimate=pl.CostEstimate(
            flops=2 * 17 * 65536 * steps * columns, bytes_accessed=2**20, transcendentals=0
        ),
    )(place, rays, target, *weights, *carried)


def local(
    features,
    spacing,
    counts,
    depth_rank,
    target,
    first_weight,
    first_bias,
    second_weight,
    second_bias,
    last_weight,
    last_bias,
):
    regions = lax.axis_size("depth")
    chips = regions * lax.axis_size("chip")
    rays = features.shape[-1]
    lanes = rays // regions // PARTS
    place = jnp.stack([jnp.bitwise_xor(depth_rank[0, 0], lax.axis_index("depth")), lax.axis_index("core")])

    got = []
    for i in range(PARTS):
        sent = pl.pallas_call(
            functools.partial(send_kernel, PARTS, i),
            in_specs=[vmem] * 3,
            out_specs=vmem,
            out_shape=shaped(regions, HEIGHT, lanes),
            cost_estimate=pl.CostEstimate(flops=0, bytes_accessed=2**20, transcendentals=0),
        )(
            features[0, 0].transpose(1, 0, 2).reshape(SAMPLES * FEAT, rays),
            spacing[0, 0].reshape(SAMPLES, rays // 128, 128),
            counts[0, 0].reshape(rays // 128, 128),
        )
        got.append(lax.all_to_all(sent, "depth", 0, 0))
    weights = prepare_weights(first_weight, first_bias, second_weight, second_bias, last_weight, last_bias)
    carried = []
    for i in range(PARTS):
        goal = target[0, :, i * lanes : (i + 1) * lanes]
        carried = step(i == 0, i == PARTS - 1, place, got[i], goal, weights, carried)
    pixels, keep, send = carried

    swap = [(0, 1), (1, 0)]
    axes = ("chip", "depth")
    half = keep + lax.ppermute(send, "core", swap)
    shares = lax.all_to_all(half.reshape(chips, PACKED // chips, 128), axes, 0, 0)
    share = jnp.sum(shares, axis=0)
    own = lax.all_to_all(jnp.broadcast_to(share[None], shares.shape), axes, 0, 0).reshape(PACKED, 128)
    other = lax.ppermute(own, "core", swap)
    first_u, first_s, second_u, second_s, last_u, last_s = pl.pallas_call(
        finish_kernel,
        in_specs=[pl.BlockSpec(memory_space=pltpu.SMEM), vmem, vmem],
        out_specs=[vmem] * 6,
        out_shape=[
            shaped(FEAT, HIDDEN),
            shaped(1, HIDDEN),
            shaped(HIDDEN, HIDDEN),
            shaped(1, HIDDEN),
            shaped(OUT, HIDDEN),
            shaped(1, OUT),
        ],
        compiler_params=pltpu.CompilerParams(vmem_limit_bytes=8 * 2**20),
    )(place, own, other)
    return (pixels[None], first_u, first_s[0], second_u, second_s[0], last_u.T, last_s[0])


def solution(mesh):
    views, regions = mesh.devices.shape
    cores = 2
    mesh = Mesh(mesh.devices.reshape(views // cores, cores, regions), ("chip", "core", "depth"))
    view = ("chip", "core")
    return jax.shard_map(
        local,
        mesh=mesh,
        in_specs=(
            P(view, "depth", None, None, None),
            P(view, "depth", None, None),
            P(view, "depth", None),
            P(view, "depth"),
            P(view, None, "depth"),
            P(),
            P(),
            P(),
            P(),
            P(),
            P(),
        ),
        out_specs=(P(view, None, "depth"), P(), P(), P(), P(), P(), P()),
        check_vma=False,
    )
```

```python
import functools

import jax
import jax.numpy as jnp
from jax import lax
from jax.experimental import pallas as pl
from jax.experimental.pallas import tpu as pltpu
from jax.sharding import Mesh
from jax.sharding import PartitionSpec as P

epsilon = 1e-05
f32 = jnp.float32
bf16 = jnp.bfloat16
FEAT, HIDDEN, CHANNELS, SAMPLES = 32, 256, 64, 3
OUT = CHANNELS + 1
OUT_ROWS = 80
ONES = 16
HEIGHT = 104
PARTS = 2
TOGETHER = 4
UNROLL = 2
WIDTH = 512
PACKED = 512


def split(value):
    high = value.astype(bf16)
    return high, (value - high.astype(f32)).astype(bf16)


def dot(left, right):
    return lax.dot_general(left, right, (((1,), (0,)), ((), ())), preferred_element_type=f32)


def dot_columns(left, right):
    return lax.dot_general(left, right, (((1,), (1,)), ((), ())), preferred_element_type=f32)


def sigmoid(value):
    return 0.5 * jnp.tanh(0.5 * value) + 0.5


def send_kernel(parts, i, features_ref, spacing_ref, counts_ref, sent_ref):
    regions, _, lanes = sent_ref.shape
    wide = lanes // 128
    lengths = [jnp.where(counts_ref[...] > s, spacing_ref[s], 0.0) for s in range(SAMPLES)]
    for j in range(regions):
        start = (j * parts + i) * lanes
        sent_ref[j, : SAMPLES * FEAT, :] = features_ref[:, start : start + lanes]
        row = (j * parts + i) * wide
        for k in range(wide):
            sent_ref[j, SAMPLES * FEAT :, k * 128 : (k + 1) * 128] = jnp.concatenate(
                [v[row + k : row + k + 1] for v in lengths]
                + [jnp.zeros((HEIGHT - SAMPLES * FEAT - SAMPLES, 128), f32)],
                axis=0,
            )


def weights_kernel(
    first_ref,
    first_bias_ref,
    second_ref,
    second_bias_ref,
    last_t_ref,
    last_bias_ref,
    first_k,
    second_k,
    second_tk,
    second_b,
    last_k,
    last_thl,
    last_b,
):
    def column(row, size):
        return jnp.transpose(jnp.broadcast_to(row, (8, size)))[:, 0:1]

    high, low = split(jnp.transpose(first_ref[...]))
    bias = column(first_bias_ref[...], HIDDEN)
    bias_h = bias.astype(bf16)
    rest = bias - bias_h.astype(f32)
    bias_m = rest.astype(bf16)
    bias_l = (rest - bias_m.astype(f32)).astype(bf16)
    pad = jnp.zeros((HIDDEN, ONES - 3), bf16)
    first_k[...] = jnp.concatenate([high, high, low, bias_h, bias_m, bias_l, pad], axis=1)
    high, low = split(second_ref[...])
    second_k[...] = jnp.concatenate([high, low], axis=1)
    high, low = split(jnp.transpose(second_ref[...]))
    second_tk[...] = jnp.concatenate([high, low, high], axis=1)
    second_b[...] = column(second_bias_ref[...], HIDDEN)
    last_t = jnp.concatenate([last_t_ref[...], jnp.zeros((128 - OUT, HIDDEN), f32)], axis=0)
    high, low = split(last_t[:OUT_ROWS])
    last_thl[...] = jnp.concatenate([high, low], axis=0)
    high, low = split(jnp.transpose(last_t)[:, :OUT_ROWS])
    last_k[...] = jnp.concatenate([high, high, low], axis=1)
    row = jnp.concatenate([last_bias_ref[...], jnp.zeros((1, 128 - OUT), f32)], axis=1)
    last_b[...] = column(row, 128)[:OUT_ROWS]


def step_kernel(first, final, place_ref, rays_ref, target_ref, *refs):
    first_k, second_k, second_tk, second_b, last_k, last_thl, last_b = refs[:7]
    refs = refs[7:]
    if not first:
        pixels_in, grad1_in, grad2_in, grad3_in, bias3_in = refs[:5]
        refs = refs[5:]
    if final:
        pixels_ref, keep_ref, send_ref = refs[:3]
        grad1, grad2, grad3, bias3 = refs[3:7]
        refs = refs[7:]
    else:
        pixels_ref, grad1, grad2, grad3, bias3 = refs[:5]
        refs = refs[5:]
    act1_h, act1_l, act2_h, act2_l, colors, rows, misfit_ref, logit, d3_hl, d2_h, d1_h = refs
    regions, _, segment = rays_ref.shape
    flip = place_ref[0]
    pieces = [(g, s) for g in range(TOGETHER) for s in range(SAMPLES)]
    columns = len(pieces) * segment

    if first:
        grad1[...] = jnp.zeros_like(grad1)
        grad2[...] = jnp.zeros_like(grad2)
        grad3[...] = jnp.zeros_like(grad3)
        bias3[...] = jnp.zeros_like(bias3)
    else:
        grad1[...] = grad1_in[...]
        grad2[...] = grad2_in[...]
        grad3[...] = grad3_in[...]
        bias3[...] = bias3_in[...]
    misfit_ref[...] = jnp.zeros_like(misfit_ref)
    def part(value, g, s):
        start = (g * SAMPLES + s) * segment
        return value[:, start : start + segment]

    def region(step, g):
        return jnp.bitwise_xor(step * TOGETHER + g, flip)

    per = WIDTH // segment
    tiles = columns // WIDTH

    def inputs(step, tile):
        x = [
            rays_ref[region(step, g), s * FEAT : (s + 1) * FEAT, :]
            for g, s in pieces[tile * per : (tile + 1) * per]
        ]
        return split(jnp.concatenate(x, axis=1))

    def at(tile):
        return slice(tile * WIDTH, (tile + 1) * WIDTH)

    def forward(step, cum):
        ones = jnp.ones((ONES, WIDTH), bf16)

        def first_layer(tile):
            xh, xl = inputs(step, tile)
            a1 = jnp.maximum(dot(first_k[...], jnp.concatenate([xh, xl, xh, ones], axis=0)), 0.0)
            a1h, a1l = split(a1)
            act1_h[step, :HIDDEN, at(tile)] = a1h
            act1_h[step, HIDDEN:, at(tile)] = ones
            act1_l[step, :, at(tile)] = a1l

        def second_layer(tile):
            a1h = act1_h[step, :HIDDEN, at(tile)]
            z2 = dot(second_tk[...], jnp.concatenate([a1h, a1h, act1_l[step, :, at(tile)]], axis=0))
            a2h, a2l = split(jnp.maximum(z2 + second_b[...], 0.0))
            act2_h[step, :, at(tile)] = a2h
            act2_l[step, :, at(tile)] = a2l

        def last_layer(tile):
            both = dot(last_thl[...], act2_h[step, :, at(tile)])
            low = dot(last_thl[:OUT_ROWS], act2_l[step, :, at(tile)])
            raw = both[:OUT_ROWS] + (both[OUT_ROWS:] + low) + last_b[...]
            colors[step, :, at(tile)] = sigmoid(raw[:CHANNELS])
            logit[:, at(tile)] = raw[CHANNELS : CHANNELS + 8]

        for stage in (first_layer, second_layer, last_layer):
            for tile in range(tiles):
                stage(tile)
        t = logit[0:1]
        density = jnp.maximum(t, 0.0) + jnp.log1p(jnp.exp(-jnp.abs(t)))
        slope = sigmoid(t)
        image = misfit_ref[...]
        for g in range(TOGETHER):
            d = region(step, g)
            passed = jnp.exp(-cum)
            before = jnp.ones_like(cum)
            total = jnp.zeros_like(cum)
            rows[step, g, 9:10, :] = passed
            for s in range(SAMPLES):
                i = g * SAMPLES + s
                length = rays_ref[d, SAMPLES * FEAT + s : SAMPLES * FEAT + s + 1, :]
                optical = part(density, g, s) * length
                weight = before * (1.0 - jnp.exp(-optical))
                total = total + optical
                before = jnp.exp(-total)
                image = image + (passed * weight) * colors[step, :, i * segment : (i + 1) * segment]
                rows[step, g, s : s + 1, :] = weight
                rows[step, g, SAMPLES + s : SAMPLES + s + 1, :] = before
                rows[step, g, 2 * SAMPLES + s : 2 * SAMPLES + s + 1, :] = part(slope, g, s) * length
            cum = cum + total
        misfit_ref[...] = image
        return cum

    steps = regions // TOGETHER
    lax.fori_loop(0, steps, forward, jnp.zeros((1, segment), f32), unroll=UNROLL)
    pixels = misfit_ref[...]
    misfit_ref[...] = pixels - target_ref[...]
    if first:
        pixels_ref[...] = pixels
    else:
        pixels_ref[...] = jnp.concatenate([pixels_in[...], pixels], axis=1)

    def backward(turn, behind):
        step = steps - 1 - turn
        misfit = misfit_ref[...]
        slopes = [None] * len(pieces)
        parts = [None] * len(pieces)
        for g in reversed(range(TOGETHER)):
            passed = rows[step, g, 9:10, :]
            later = -behind
            for s in reversed(range(SAMPLES)):
                i = g * SAMPLES + s
                weight = rows[step, g, s : s + 1, :]
                after = rows[step, g, SAMPLES + s : SAMPLES + s + 1, :]
                sc = colors[step, :, i * segment : (i + 1) * segment]
                product = misfit * sc
                value = passed * jnp.sum(product, axis=0, keepdims=True)
                parts[i] = (passed * weight) * (product - product * sc)
                slopes[i] = (value * after + later) * rows[step, g, 2 * SAMPLES + s : 2 * SAMPLES + s + 1, :]
                later = later - weight * value
            behind = -later
        def output(tile):
            mine = slice(tile * per, (tile + 1) * per)
            d3 = jnp.concatenate(
                [
                    jnp.concatenate(parts[mine], axis=1),
                    jnp.concatenate(slopes[mine], axis=1),
                    jnp.zeros((OUT_ROWS - OUT, WIDTH), f32),
                ],
                axis=0,
            )
            high, low = split(d3)
            d3_hl[:OUT_ROWS, at(tile)] = high
            d3_hl[OUT_ROWS:, at(tile)] = low
            bias3[...] += sum(d3[:, i * segment : (i + 1) * segment] for i in range(per))

        def last_layer(tile):
            d3h = d3_hl[:OUT_ROWS, at(tile)]
            d2 = dot(last_k[...], jnp.concatenate([d3h, d3_hl[OUT_ROWS:, at(tile)], d3h], axis=0)).astype(bf16)
            d2_h[:, at(tile)] = jnp.where(act2_h[step, :, at(tile)] > 0, d2, jnp.zeros_like(d2))

        def second_layer(tile):
            high = d2_h[:, at(tile)]
            d1 = dot(second_k[...], jnp.concatenate([high, high], axis=0)).astype(bf16)
            d1_h[:, at(tile)] = jnp.where(act1_h[step, :HIDDEN, at(tile)] > 0, d1, jnp.zeros_like(d1))

        def sum_last():
            d3h = d3_hl[:OUT_ROWS]
            grad3[...] += dot_columns(d3h, act2_h[step]) + dot_columns(d3h, act2_l[step])

        def sum_second():
            a1h = act1_h[step]
            grad2[...] += dot_columns(a1h, d2_h[...])
            grad2[:HIDDEN] += dot_columns(act1_l[step], d2_h[...])

        def sum_first():
            x = [inputs(step, tile) for tile in range(tiles)]
            xh = jnp.concatenate([h for h, _ in x], axis=1)
            xl = jnp.concatenate([l for _, l in x], axis=1)
            ones = jnp.ones((ONES, columns), bf16)
            both = dot_columns(jnp.concatenate([xh, ones, xl], axis=0), d1_h[...])
            grad1[...] += both[: FEAT + ONES]
            grad1[:FEAT] += both[FEAT + ONES :]

        for stage in (output, last_layer, second_layer):
            for tile in range(tiles):
                stage(tile)
        sum_last()
        sum_second()
        sum_first()
        return behind

    lax.fori_loop(0, steps, backward, jnp.zeros((1, segment), f32), unroll=UNROLL)
    if not final:
        return

    half = HIDDEN // 2
    third = lax.dot_general(
        jnp.ones((8, segment), f32),
        jnp.concatenate([bias3[...], jnp.zeros((half - OUT_ROWS, segment), f32)], axis=0),
        (((1,), (1,)), ((), ())),
        precision=lax.Precision.HIGHEST,
        preferred_element_type=f32,
    )

    def pack(hidden_ref, others_ref):
        for side in range(2):
            lanes = slice(side * half, (side + 1) * half)
            hidden_ref[side * 256 : side * 256 + 256] = grad2[:HIDDEN, lanes]
            others_ref[side * 32 : 32 + side * 32] = grad1[:FEAT, lanes]
            others_ref[64 + side * 80 : 144 + side * 80] = grad3[:, lanes]
            misc = [grad1[FEAT : FEAT + 1, lanes], grad2[HIDDEN : HIDDEN + 1, lanes], third[0:1]]
            others_ref[224 + side * 8 : 232 + side * 8] = jnp.concatenate(misc + [jnp.zeros((5, half), f32)], axis=0)
        others_ref[240:] = jnp.zeros((PACKED - 240, half), f32)

    @pl.when(place_ref[1] == 0)
    def _():
        pack(keep_ref, send_ref)

    @pl.when(place_ref[1] == 1)
    def _():
        pack(send_ref, keep_ref)


def finish_kernel(place_ref, own_ref, other_ref, first_ref, first_b_ref, second_ref, second_b_ref, last_t_ref, last_b_ref):
    def scale(parts, count):
        squares = sum(jnp.sum(part * part, keepdims=True) for part in parts)
        return 1.0 / jnp.sqrt(squares / count + epsilon)

    def finish(hidden_ref, others_ref):
        def both(ref, start, rows, stride):
            return [ref[start : start + rows, :], ref[start + stride : start + stride + rows, :]]

        parts = both(hidden_ref, 0, 256, 256)
        second_ref[...] = jnp.concatenate(parts, axis=1) * scale(parts, HIDDEN * HIDDEN)
        parts = both(others_ref, 0, 32, 32)
        first_ref[...] = jnp.concatenate(parts, axis=1) * scale(parts, FEAT * HIDDEN)
        parts = both(others_ref, 64, 80, 80)
        last_t_ref[...] = jnp.concatenate(parts, axis=1)[:OUT] * scale(parts, HIDDEN * OUT)
        parts = both(others_ref, 224, 1, 8)
        first_b_ref[...] = jnp.concatenate(parts, axis=1) * scale(parts, HIDDEN)
        parts = both(others_ref, 225, 1, 8)
        second_b_ref[...] = jnp.concatenate(parts, axis=1) * scale(parts, HIDDEN)
        part = others_ref[226:227, :]
        last_b_ref[...] = (part * scale([part], OUT))[:, :OUT]

    @pl.when(place_ref[1] == 0)
    def _():
        finish(own_ref, other_ref)

    @pl.when(place_ref[1] == 1)
    def _():
        finish(other_ref, own_ref)


vmem = pl.BlockSpec(memory_space=pltpu.VMEM)


def shaped(*shape, dtype=f32):
    return jax.ShapeDtypeStruct(shape, dtype)


def prepare_weights(first_weight, first_bias, second_weight, second_bias, last_weight, last_bias):
    return pl.pallas_call(
        weights_kernel,
        in_specs=[vmem] * 6,
        out_specs=[vmem] * 7,
        out_shape=[
            shaped(HIDDEN, 3 * FEAT + ONES, dtype=bf16),
            shaped(HIDDEN, 2 * HIDDEN, dtype=bf16),
            shaped(HIDDEN, 3 * HIDDEN, dtype=bf16),
            shaped(HIDDEN, 1),
            shaped(HIDDEN, 3 * OUT_ROWS, dtype=bf16),
            shaped(2 * OUT_ROWS, HIDDEN, dtype=bf16),
            shaped(OUT_ROWS, 1),
        ],
        compiler_params=pltpu.CompilerParams(vmem_limit_bytes=8 * 2**20),
    )(first_weight, first_bias[None], second_weight, second_bias[None], last_weight.T, last_bias[None])


def step(first, final, place, rays, target, weights, carried):
    regions, _, segment = rays.shape
    columns = TOGETHER * SAMPLES * segment
    steps = regions // TOGETHER
    sums = [
        shaped(FEAT + ONES, HIDDEN),
        shaped(HIDDEN + ONES, HIDDEN),
        shaped(OUT_ROWS, HIDDEN),
        shaped(OUT_ROWS, segment),
    ]
    scratch = [
        pltpu.VMEM((steps, HIDDEN + ONES, columns), bf16),
        pltpu.VMEM((steps, HIDDEN, columns), bf16),
        pltpu.VMEM((steps, HIDDEN, columns), bf16),
        pltpu.VMEM((steps, HIDDEN, columns), bf16),
        pltpu.VMEM((steps, CHANNELS, columns), f32),
        pltpu.VMEM((steps, TOGETHER, 16, segment), f32),
        pltpu.VMEM((CHANNELS, segment), f32),
        pltpu.VMEM((8, columns), f32),
        pltpu.VMEM((2 * OUT_ROWS, columns), bf16),
        pltpu.VMEM((HIDDEN, columns), bf16),
        pltpu.VMEM((HIDDEN, columns), bf16),
    ]
    width = segment if first else 2 * segment
    if final:
        out_shape = [shaped(CHANNELS, width), shaped(PACKED, 128), shaped(PACKED, 128)]
        scratch = [pltpu.VMEM(s.shape, f32) for s in sums] + scratch
    else:
        out_shape = [shaped(CHANNELS, width)] + sums
    return pl.pallas_call(
        functools.partial(step_kernel, first, final),
        in_specs=[pl.BlockSpec(memory_space=pltpu.SMEM)] + [vmem] * (2 + len(weights) + len(carried)),
        out_specs=[vmem] * len(out_shape),
        out_shape=out_shape,
        scratch_shapes=scratch,
        compiler_params=pltpu.CompilerParams(vmem_limit_bytes=44 * 2**20),
        cost_estimate=pl.CostEstimate(
            flops=2 * 17 * 65536 * steps * columns, bytes_accessed=2**20, transcendentals=0
        ),
    )(place, rays, target, *weights, *carried)


def local(
    features,
    spacing,
    counts,
    depth_rank,
    target,
    first_weight,
    first_bias,
    second_weight,
    second_bias,
    last_weight,
    last_bias,
):
    regions = lax.axis_size("depth")
    chips = regions * lax.axis_size("chip")
    rays = features.shape[-1]
    lanes = rays // regions // PARTS
    place = jnp.stack([jnp.bitwise_xor(depth_rank[0, 0], lax.axis_index("depth")), lax.axis_index("core")])

    got = []
    for i in range(PARTS):
        sent = pl.pallas_call(
            functools.partial(send_kernel, PARTS, i),
            in_specs=[vmem] * 3,
            out_specs=vmem,
            out_shape=shaped(regions, HEIGHT, lanes),
            cost_estimate=pl.CostEstimate(flops=0, bytes_accessed=2**20, transcendentals=0),
        )(
            features[0, 0].transpose(1, 0, 2).reshape(SAMPLES * FEAT, rays),
            spacing[0, 0].reshape(SAMPLES, rays // 128, 128),
            counts[0, 0].reshape(rays // 128, 128),
        )
        got.append(lax.all_to_all(sent, "depth", 0, 0))
    weights = prepare_weights(first_weight, first_bias, second_weight, second_bias, last_weight, last_bias)
    carried = []
    for i in range(PARTS):
        goal = target[0, :, i * lanes : (i + 1) * lanes]
        carried = step(i == 0, i == PARTS - 1, place, got[i], goal, weights, carried)
    pixels, keep, send = carried

    swap = [(0, 1), (1, 0)]
    axes = ("chip", "depth")
    half = keep + lax.ppermute(send, "core", swap)
    shares = lax.all_to_all(half.reshape(chips, PACKED // chips, 128), axes, 0, 0)
    share = jnp.sum(shares, axis=0)
    own = lax.all_to_all(jnp.broadcast_to(share[None], shares.shape), axes, 0, 0).reshape(PACKED, 128)
    other = lax.ppermute(own, "core", swap)
    first_u, first_s, second_u, second_s, last_u, last_s = pl.pallas_call(
        finish_kernel,
        in_specs=[pl.BlockSpec(memory_space=pltpu.SMEM), vmem, vmem],
        out_specs=[vmem] * 6,
        out_shape=[
            shaped(FEAT, HIDDEN),
            shaped(1, HIDDEN),
            shaped(HIDDEN, HIDDEN),
            shaped(1, HIDDEN),
            shaped(OUT, HIDDEN),
            shaped(1, OUT),
        ],
        compiler_params=pltpu.CompilerParams(vmem_limit_bytes=8 * 2**20),
    )(place, own, other)
    return (pixels[None], first_u, first_s[0], second_u, second_s[0], last_u.T, last_s[0])


def solution(mesh):
    views, regions = mesh.devices.shape
    cores = 2
    mesh = Mesh(mesh.devices.reshape(views // cores, cores, regions), ("chip", "core", "depth"))
    view = ("chip", "core")
    return jax.shard_map(
        local,
        mesh=mesh,
        in_specs=(
            P(view, "depth", None, None, None),
            P(view, "depth", None, None),
            P(view, "depth", None),
            P(view, "depth"),
            P(view, None, "depth"),
            P(),
            P(),
            P(),
            P(),
            P(),
            P(),
        ),
        out_specs=(P(view, None, "depth"), P(), P(), P(), P(), P(), P()),
        check_vma=False,
    )
```

```python
import functools

import jax
import jax.numpy as jnp
from jax import lax
from jax.experimental import pallas as pl
from jax.experimental.pallas import tpu as pltpu
from jax.sharding import Mesh
from jax.sharding import PartitionSpec as P

epsilon = 1e-05
f32 = jnp.float32
bf16 = jnp.bfloat16
FEAT, HIDDEN, CHANNELS, SAMPLES = 32, 256, 64, 3
OUT = CHANNELS + 1
OUT_ROWS = 80
ONES = 16
HEIGHT = 104
PARTS = 2
TOGETHER = 4
UNROLL = 2
WIDTH = 512
PACKED = 512


def split(value):
    high = value.astype(bf16)
    return high, (value - high.astype(f32)).astype(bf16)


def dot(left, right):
    return lax.dot_general(left, right, (((1,), (0,)), ((), ())), preferred_element_type=f32)


def dot_columns(left, right):
    return lax.dot_general(left, right, (((1,), (1,)), ((), ())), preferred_element_type=f32)


def sigmoid(value):
    return 0.5 * jnp.tanh(0.5 * value) + 0.5


def send_kernel(parts, i, features_ref, spacing_ref, counts_ref, sent_ref):
    regions, _, lanes = sent_ref.shape
    wide = lanes // 128
    lengths = [jnp.where(counts_ref[...] > s, spacing_ref[s], 0.0) for s in range(SAMPLES)]
    for j in range(regions):
        start = (j * parts + i) * lanes
        sent_ref[j, : SAMPLES * FEAT, :] = features_ref[:, start : start + lanes]
        row = (j * parts + i) * wide
        for k in range(wide):
            sent_ref[j, SAMPLES * FEAT :, k * 128 : (k + 1) * 128] = jnp.concatenate(
                [v[row + k : row + k + 1] for v in lengths]
                + [jnp.zeros((HEIGHT - SAMPLES * FEAT - SAMPLES, 128), f32)],
                axis=0,
            )


def weights_kernel(
    first_ref,
    first_bias_ref,
    second_ref,
    second_bias_ref,
    last_t_ref,
    last_bias_ref,
    first_k,
    second_k,
    second_tk,
    second_b,
    last_k,
    last_thl,
    last_b,
):
    def column(row, size):
        return jnp.transpose(jnp.broadcast_to(row, (8, size)))[:, 0:1]

    high, low = split(jnp.transpose(first_ref[...]))
    bias = column(first_bias_ref[...], HIDDEN)
    bias_h = bias.astype(bf16)
    rest = bias - bias_h.astype(f32)
    bias_m = rest.astype(bf16)
    bias_l = (rest - bias_m.astype(f32)).astype(bf16)
    pad = jnp.zeros((HIDDEN, ONES - 3), bf16)
    first_k[...] = jnp.concatenate([high, high, low, bias_h, bias_m, bias_l, pad], axis=1)
    high, low = split(second_ref[...])
    second_k[...] = jnp.concatenate([high, low], axis=1)
    high, low = split(jnp.transpose(second_ref[...]))
    second_tk[...] = jnp.concatenate([high, low, high], axis=1)
    second_b[...] = column(second_bias_ref[...], HIDDEN)
    last_t = jnp.concatenate([last_t_ref[...], jnp.zeros((128 - OUT, HIDDEN), f32)], axis=0)
    high, low = split(last_t[:OUT_ROWS])
    last_thl[...] = jnp.concatenate([high, low], axis=0)
    high, low = split(jnp.transpose(last_t)[:, :OUT_ROWS])
    last_k[...] = jnp.concatenate([high, high, low], axis=1)
    row = jnp.concatenate([last_bias_ref[...], jnp.zeros((1, 128 - OUT), f32)], axis=1)
    last_b[...] = column(row, 128)[:OUT_ROWS]


def step_kernel(first, final, place_ref, rays_ref, target_ref, *refs):
    first_k, second_k, second_tk, second_b, last_k, last_thl, last_b = refs[:7]
    refs = refs[7:]
    if not first:
        pixels_in, grad1_in, grad2_in, grad3_in, bias3_in = refs[:5]
        refs = refs[5:]
    if final:
        pixels_ref, keep_ref, send_ref = refs[:3]
        grad1, grad2, grad3, bias3 = refs[3:7]
        refs = refs[7:]
    else:
        pixels_ref, grad1, grad2, grad3, bias3 = refs[:5]
        refs = refs[5:]
    act1_h, act1_l, act2_h, act2_l, colors, rows, misfit_ref, logit, d3_hl, d2_h, d1_h = refs
    regions, _, segment = rays_ref.shape
    flip = place_ref[0]
    pieces = [(g, s) for g in range(TOGETHER) for s in range(SAMPLES)]
    columns = len(pieces) * segment

    if first:
        grad1[...] = jnp.zeros_like(grad1)
        grad2[...] = jnp.zeros_like(grad2)
        grad3[...] = jnp.zeros_like(grad3)
        bias3[...] = jnp.zeros_like(bias3)
    else:
        grad1[...] = grad1_in[...]
        grad2[...] = grad2_in[...]
        grad3[...] = grad3_in[...]
        bias3[...] = bias3_in[...]
    misfit_ref[...] = jnp.zeros_like(misfit_ref)
    def part(value, g, s):
        start = (g * SAMPLES + s) * segment
        return value[:, start : start + segment]

    def region(step, g):
        return jnp.bitwise_xor(step * TOGETHER + g, flip)

    per = WIDTH // segment
    tiles = columns // WIDTH

    def inputs(step, tile):
        x = [
            rays_ref[region(step, g), s * FEAT : (s + 1) * FEAT, :]
            for g, s in pieces[tile * per : (tile + 1) * per]
        ]
        return split(jnp.concatenate(x, axis=1))

    def at(tile):
        return slice(tile * WIDTH, (tile + 1) * WIDTH)

    def forward(step, cum):
        ones = jnp.ones((ONES, WIDTH), bf16)
        slot = step % 2

        def first_layer(tile):
            xh, xl = inputs(step, tile)
            a1 = jnp.maximum(dot(first_k[...], jnp.concatenate([xh, xl, xh, ones], axis=0)), 0.0)
            a1h, a1l = split(a1)
            act1_h[step, :HIDDEN, at(tile)] = a1h
            act1_h[step, HIDDEN:, at(tile)] = ones
            act1_l[slot, :, at(tile)] = a1l

        def second_layer(tile):
            a1h = act1_h[step, :HIDDEN, at(tile)]
            z2 = dot(second_tk[...], jnp.concatenate([a1h, a1h, act1_l[slot, :, at(tile)]], axis=0))
            a2h, a2l = split(jnp.maximum(z2 + second_b[...], 0.0))
            act2_h[step, :, at(tile)] = a2h
            act2_l[slot, :, at(tile)] = a2l

        def last_layer(tile):
            both = dot(last_thl[...], act2_h[step, :, at(tile)])
            low = dot(last_thl[:OUT_ROWS], act2_l[slot, :, at(tile)])
            raw = both[:OUT_ROWS] + (both[OUT_ROWS:] + low) + last_b[...]
            colors[step, :, at(tile)] = sigmoid(raw[:CHANNELS])
            logit[:, at(tile)] = raw[CHANNELS : CHANNELS + 8]

        for stage in (first_layer, second_layer, last_layer):
            for tile in range(tiles):
                stage(tile)
        t = logit[0:1]
        density = jnp.maximum(t, 0.0) + jnp.log1p(jnp.exp(-jnp.abs(t)))
        slope = sigmoid(t)
        image = misfit_ref[...]
        for g in range(TOGETHER):
            d = region(step, g)
            passed = jnp.exp(-cum)
            before = jnp.ones_like(cum)
            total = jnp.zeros_like(cum)
            rows[step, g, 9:10, :] = passed
            for s in range(SAMPLES):
                i = g * SAMPLES + s
                length = rays_ref[d, SAMPLES * FEAT + s : SAMPLES * FEAT + s + 1, :]
                optical = part(density, g, s) * length
                weight = before * (1.0 - jnp.exp(-optical))
                total = total + optical
                before = jnp.exp(-total)
                image = image + (passed * weight) * colors[step, :, i * segment : (i + 1) * segment]
                rows[step, g, s : s + 1, :] = weight
                rows[step, g, SAMPLES + s : SAMPLES + s + 1, :] = before
                rows[step, g, 2 * SAMPLES + s : 2 * SAMPLES + s + 1, :] = part(slope, g, s) * length
            cum = cum + total
        misfit_ref[...] = image
        return cum

    steps = regions // TOGETHER
    lax.fori_loop(0, steps, forward, jnp.zeros((1, segment), f32), unroll=UNROLL)
    pixels = misfit_ref[...]
    misfit_ref[...] = pixels - target_ref[...]
    if first:
        pixels_ref[...] = pixels
    else:
        pixels_ref[...] = jnp.concatenate([pixels_in[...], pixels], axis=1)

    def backward(turn, behind):
        step = steps - 1 - turn
        misfit = misfit_ref[...]
        slopes = [None] * len(pieces)
        parts = [None] * len(pieces)
        for g in reversed(range(TOGETHER)):
            passed = rows[step, g, 9:10, :]
            later = -behind
            for s in reversed(range(SAMPLES)):
                i = g * SAMPLES + s
                weight = rows[step, g, s : s + 1, :]
                after = rows[step, g, SAMPLES + s : SAMPLES + s + 1, :]
                sc = colors[step, :, i * segment : (i + 1) * segment]
                product = misfit * sc
                value = passed * jnp.sum(product, axis=0, keepdims=True)
                parts[i] = (passed * weight) * (product - product * sc)
                slopes[i] = (value * after + later) * rows[step, g, 2 * SAMPLES + s : 2 * SAMPLES + s + 1, :]
                later = later - weight * value
            behind = -later
        def output(tile):
            mine = slice(tile * per, (tile + 1) * per)
            d3 = jnp.concatenate(
                [
                    jnp.concatenate(parts[mine], axis=1),
                    jnp.concatenate(slopes[mine], axis=1),
                    jnp.zeros((OUT_ROWS - OUT, WIDTH), f32),
                ],
                axis=0,
            )
            high, low = split(d3)
            d3_hl[:OUT_ROWS, at(tile)] = high
            d3_hl[OUT_ROWS:, at(tile)] = low
            bias3[...] += sum(d3[:, i * segment : (i + 1) * segment] for i in range(per))

        def last_layer(tile):
            d3h = d3_hl[:OUT_ROWS, at(tile)]
            d2 = dot(last_k[...], jnp.concatenate([d3h, d3_hl[OUT_ROWS:, at(tile)], d3h], axis=0)).astype(bf16)
            d2_h[:, at(tile)] = jnp.where(act2_h[step, :, at(tile)] > 0, d2, jnp.zeros_like(d2))

        def second_layer(tile):
            high = d2_h[:, at(tile)]
            d1 = dot(second_k[...], jnp.concatenate([high, high], axis=0)).astype(bf16)
            d1_h[:, at(tile)] = jnp.where(act1_h[step, :HIDDEN, at(tile)] > 0, d1, jnp.zeros_like(d1))

        def sum_last():
            grad3[...] += dot_columns(d3_hl[:OUT_ROWS], act2_h[step])

        def sum_second():
            grad2[...] += dot_columns(act1_h[step], d2_h[...])

        def sum_first():
            x = [inputs(step, tile) for tile in range(tiles)]
            xh = jnp.concatenate([h for h, _ in x], axis=1)
            xl = jnp.concatenate([l for _, l in x], axis=1)
            ones = jnp.ones((ONES, columns), bf16)
            both = dot_columns(jnp.concatenate([xh, ones, xl], axis=0), d1_h[...])
            grad1[...] += both[: FEAT + ONES]
            grad1[:FEAT] += both[FEAT + ONES :]

        for stage in (output, last_layer, second_layer):
            for tile in range(tiles):
                stage(tile)
        sum_last()
        sum_second()
        sum_first()
        return behind

    lax.fori_loop(0, steps, backward, jnp.zeros((1, segment), f32), unroll=UNROLL)
    if not final:
        return

    half = HIDDEN // 2
    third = lax.dot_general(
        jnp.ones((8, segment), f32),
        jnp.concatenate([bias3[...], jnp.zeros((half - OUT_ROWS, segment), f32)], axis=0),
        (((1,), (1,)), ((), ())),
        precision=lax.Precision.HIGHEST,
        preferred_element_type=f32,
    )

    def pack(hidden_ref, others_ref):
        for side in range(2):
            lanes = slice(side * half, (side + 1) * half)
            hidden_ref[side * 256 : side * 256 + 256] = grad2[:HIDDEN, lanes]
            others_ref[side * 32 : 32 + side * 32] = grad1[:FEAT, lanes]
            others_ref[64 + side * 80 : 144 + side * 80] = grad3[:, lanes]
            misc = [grad1[FEAT : FEAT + 1, lanes], grad2[HIDDEN : HIDDEN + 1, lanes], third[0:1]]
            others_ref[224 + side * 8 : 232 + side * 8] = jnp.concatenate(misc + [jnp.zeros((5, half), f32)], axis=0)
        others_ref[240:] = jnp.zeros((PACKED - 240, half), f32)

    @pl.when(place_ref[1] == 0)
    def _():
        pack(keep_ref, send_ref)

    @pl.when(place_ref[1] == 1)
    def _():
        pack(send_ref, keep_ref)


def finish_kernel(place_ref, own_ref, other_ref, first_ref, first_b_ref, second_ref, second_b_ref, last_t_ref, last_b_ref):
    def scale(parts, count):
        squares = sum(jnp.sum(part * part, keepdims=True) for part in parts)
        return 1.0 / jnp.sqrt(squares / count + epsilon)

    def finish(hidden_ref, others_ref):
        def both(ref, start, rows, stride):
            return [ref[start : start + rows, :], ref[start + stride : start + stride + rows, :]]

        parts = both(hidden_ref, 0, 256, 256)
        second_ref[...] = jnp.concatenate(parts, axis=1) * scale(parts, HIDDEN * HIDDEN)
        parts = both(others_ref, 0, 32, 32)
        first_ref[...] = jnp.concatenate(parts, axis=1) * scale(parts, FEAT * HIDDEN)
        parts = both(others_ref, 64, 80, 80)
        last_t_ref[...] = jnp.concatenate(parts, axis=1)[:OUT] * scale(parts, HIDDEN * OUT)
        parts = both(others_ref, 224, 1, 8)
        first_b_ref[...] = jnp.concatenate(parts, axis=1) * scale(parts, HIDDEN)
        parts = both(others_ref, 225, 1, 8)
        second_b_ref[...] = jnp.concatenate(parts, axis=1) * scale(parts, HIDDEN)
        part = others_ref[226:227, :]
        last_b_ref[...] = (part * scale([part], OUT))[:, :OUT]

    @pl.when(place_ref[1] == 0)
    def _():
        finish(own_ref, other_ref)

    @pl.when(place_ref[1] == 1)
    def _():
        finish(other_ref, own_ref)


vmem = pl.BlockSpec(memory_space=pltpu.VMEM)


def shaped(*shape, dtype=f32):
    return jax.ShapeDtypeStruct(shape, dtype)


def prepare_weights(first_weight, first_bias, second_weight, second_bias, last_weight, last_bias):
    return pl.pallas_call(
        weights_kernel,
        in_specs=[vmem] * 6,
        out_specs=[vmem] * 7,
        out_shape=[
            shaped(HIDDEN, 3 * FEAT + ONES, dtype=bf16),
            shaped(HIDDEN, 2 * HIDDEN, dtype=bf16),
            shaped(HIDDEN, 3 * HIDDEN, dtype=bf16),
            shaped(HIDDEN, 1),
            shaped(HIDDEN, 3 * OUT_ROWS, dtype=bf16),
            shaped(2 * OUT_ROWS, HIDDEN, dtype=bf16),
            shaped(OUT_ROWS, 1),
        ],
        compiler_params=pltpu.CompilerParams(vmem_limit_bytes=8 * 2**20),
    )(first_weight, first_bias[None], second_weight, second_bias[None], last_weight.T, last_bias[None])


def step(first, final, place, rays, target, weights, carried):
    regions, _, segment = rays.shape
    columns = TOGETHER * SAMPLES * segment
    steps = regions // TOGETHER
    sums = [
        shaped(FEAT + ONES, HIDDEN),
        shaped(HIDDEN + ONES, HIDDEN),
        shaped(OUT_ROWS, HIDDEN),
        shaped(OUT_ROWS, segment),
    ]
    scratch = [
        pltpu.VMEM((steps, HIDDEN + ONES, columns), bf16),
        pltpu.VMEM((2, HIDDEN, columns), bf16),
        pltpu.VMEM((steps, HIDDEN, columns), bf16),
        pltpu.VMEM((2, HIDDEN, columns), bf16),
        pltpu.VMEM((steps, CHANNELS, columns), f32),
        pltpu.VMEM((steps, TOGETHER, 16, segment), f32),
        pltpu.VMEM((CHANNELS, segment), f32),
        pltpu.VMEM((8, columns), f32),
        pltpu.VMEM((2 * OUT_ROWS, columns), bf16),
        pltpu.VMEM((HIDDEN, columns), bf16),
        pltpu.VMEM((HIDDEN, columns), bf16),
    ]
    width = segment if first else 2 * segment
    if final:
        out_shape = [shaped(CHANNELS, width), shaped(PACKED, 128), shaped(PACKED, 128)]
        scratch = [pltpu.VMEM(s.shape, f32) for s in sums] + scratch
    else:
        out_shape = [shaped(CHANNELS, width)] + sums
    return pl.pallas_call(
        functools.partial(step_kernel, first, final),
        in_specs=[pl.BlockSpec(memory_space=pltpu.SMEM)] + [vmem] * (2 + len(weights) + len(carried)),
        out_specs=[vmem] * len(out_shape),
        out_shape=out_shape,
        scratch_shapes=scratch,
        compiler_params=pltpu.CompilerParams(vmem_limit_bytes=44 * 2**20),
        cost_estimate=pl.CostEstimate(
            flops=2 * 17 * 65536 * steps * columns, bytes_accessed=2**20, transcendentals=0
        ),
    )(place, rays, target, *weights, *carried)


def local(
    features,
    spacing,
    counts,
    depth_rank,
    target,
    first_weight,
    first_bias,
    second_weight,
    second_bias,
    last_weight,
    last_bias,
):
    regions = lax.axis_size("depth")
    chips = regions * lax.axis_size("chip")
    rays = features.shape[-1]
    lanes = rays // regions // PARTS
    place = jnp.stack([jnp.bitwise_xor(depth_rank[0, 0], lax.axis_index("depth")), lax.axis_index("core")])

    got = []
    for i in range(PARTS):
        sent = pl.pallas_call(
            functools.partial(send_kernel, PARTS, i),
            in_specs=[vmem] * 3,
            out_specs=vmem,
            out_shape=shaped(regions, HEIGHT, lanes),
            cost_estimate=pl.CostEstimate(flops=0, bytes_accessed=2**20, transcendentals=0),
        )(
            features[0, 0].transpose(1, 0, 2).reshape(SAMPLES * FEAT, rays),
            spacing[0, 0].reshape(SAMPLES, rays // 128, 128),
            counts[0, 0].reshape(rays // 128, 128),
        )
        got.append(lax.all_to_all(sent, "depth", 0, 0))
    weights = prepare_weights(first_weight, first_bias, second_weight, second_bias, last_weight, last_bias)
    carried = []
    for i in range(PARTS):
        goal = target[0, :, i * lanes : (i + 1) * lanes]
        carried = step(i == 0, i == PARTS - 1, place, got[i], goal, weights, carried)
    pixels, keep, send = carried

    swap = [(0, 1), (1, 0)]
    axes = ("chip", "depth")
    half = keep + lax.ppermute(send, "core", swap)
    shares = lax.all_to_all(half.reshape(chips, PACKED // chips, 128), axes, 0, 0)
    share = jnp.sum(shares, axis=0)
    own = lax.all_to_all(jnp.broadcast_to(share[None], shares.shape), axes, 0, 0).reshape(PACKED, 128)
    other = lax.ppermute(own, "core", swap)
    first_u, first_s, second_u, second_s, last_u, last_s = pl.pallas_call(
        finish_kernel,
        in_specs=[pl.BlockSpec(memory_space=pltpu.SMEM), vmem, vmem],
        out_specs=[vmem] * 6,
        out_shape=[
            shaped(FEAT, HIDDEN),
            shaped(1, HIDDEN),
            shaped(HIDDEN, HIDDEN),
            shaped(1, HIDDEN),
            shaped(OUT, HIDDEN),
            shaped(1, OUT),
        ],
        compiler_params=pltpu.CompilerParams(vmem_limit_bytes=8 * 2**20),
    )(place, own, other)
    return (pixels[None], first_u, first_s[0], second_u, second_s[0], last_u.T, last_s[0])


def solution(mesh):
    views, regions = mesh.devices.shape
    cores = 2
    mesh = Mesh(mesh.devices.reshape(views // cores, cores, regions), ("chip", "core", "depth"))
    view = ("chip", "core")
    return jax.shard_map(
        local,
        mesh=mesh,
        in_specs=(
            P(view, "depth", None, None, None),
            P(view, "depth", None, None),
            P(view, "depth", None),
            P(view, "depth"),
            P(view, None, "depth"),
            P(),
            P(),
            P(),
            P(),
            P(),
            P(),
        ),
        out_specs=(P(view, None, "depth"), P(), P(), P(), P(), P(), P()),
        check_vma=False,
    )
```

```python
import functools

import jax
import jax.numpy as jnp
from jax import lax
from jax.experimental import pallas as pl
from jax.experimental.pallas import tpu as pltpu
from jax.sharding import Mesh
from jax.sharding import PartitionSpec as P

epsilon = 1e-05
f32 = jnp.float32
bf16 = jnp.bfloat16
FEAT, HIDDEN, CHANNELS, SAMPLES = 32, 256, 64, 3
OUT = CHANNELS + 1
OUT_ROWS = 80
ONES = 16
HEIGHT = 104
PARTS = 2
TOGETHER = 4
FORWARD_UNROLL = 2
BACKWARD_UNROLL = 4
WIDTH = 512
PACKED = 512


def split(value):
    high = value.astype(bf16)
    return high, (value - high.astype(f32)).astype(bf16)


def dot(left, right):
    return lax.dot_general(left, right, (((1,), (0,)), ((), ())), preferred_element_type=f32)


def dot_columns(left, right):
    return lax.dot_general(left, right, (((1,), (1,)), ((), ())), preferred_element_type=f32)


def sigmoid(value):
    return 0.5 * jnp.tanh(0.5 * value) + 0.5


def send_kernel(parts, i, features_ref, spacing_ref, counts_ref, sent_ref):
    regions, _, lanes = sent_ref.shape
    wide = lanes // 128
    lengths = [jnp.where(counts_ref[...] > s, spacing_ref[s], 0.0) for s in range(SAMPLES)]
    for j in range(regions):
        start = (j * parts + i) * lanes
        sent_ref[j, : SAMPLES * FEAT, :] = features_ref[:, start : start + lanes]
        row = (j * parts + i) * wide
        for k in range(wide):
            sent_ref[j, SAMPLES * FEAT :, k * 128 : (k + 1) * 128] = jnp.concatenate(
                [v[row + k : row + k + 1] for v in lengths]
                + [jnp.zeros((HEIGHT - SAMPLES * FEAT - SAMPLES, 128), f32)],
                axis=0,
            )


def weights_kernel(
    first_ref,
    first_bias_ref,
    second_ref,
    second_bias_ref,
    last_t_ref,
    last_bias_ref,
    first_k,
    second_k,
    second_tk,
    second_b,
    last_k,
    last_thl,
    last_b,
):
    def column(row, size):
        return jnp.transpose(jnp.broadcast_to(row, (8, size)))[:, 0:1]

    high, low = split(jnp.transpose(first_ref[...]))
    bias = column(first_bias_ref[...], HIDDEN)
    bias_h = bias.astype(bf16)
    rest = bias - bias_h.astype(f32)
    bias_m = rest.astype(bf16)
    bias_l = (rest - bias_m.astype(f32)).astype(bf16)
    pad = jnp.zeros((HIDDEN, ONES - 3), bf16)
    first_k[...] = jnp.concatenate([high, high, low, bias_h, bias_m, bias_l, pad], axis=1)
    high, low = split(second_ref[...])
    second_k[...] = jnp.concatenate([high, low], axis=1)
    high, low = split(jnp.transpose(second_ref[...]))
    second_tk[...] = jnp.concatenate([high, low, high], axis=1)
    second_b[...] = column(second_bias_ref[...], HIDDEN)
    last_t = jnp.concatenate([last_t_ref[...], jnp.zeros((128 - OUT, HIDDEN), f32)], axis=0)
    high, low = split(last_t[:OUT_ROWS])
    last_thl[...] = jnp.concatenate([high, low], axis=0)
    high, low = split(jnp.transpose(last_t)[:, :OUT_ROWS])
    last_k[...] = jnp.concatenate([high, high, low], axis=1)
    row = jnp.concatenate([last_bias_ref[...], jnp.zeros((1, 128 - OUT), f32)], axis=1)
    last_b[...] = column(row, 128)[:OUT_ROWS]


def step_kernel(first, final, place_ref, rays_ref, target_ref, *refs):
    first_k, second_k, second_tk, second_b, last_k, last_thl, last_b = refs[:7]
    refs = refs[7:]
    if not first:
        pixels_in, grad1_in, grad2_in, grad3_in, bias3_in = refs[:5]
        refs = refs[5:]
    if final:
        pixels_ref, keep_ref, send_ref = refs[:3]
        grad1, grad2, grad3, bias3 = refs[3:7]
        refs = refs[7:]
    else:
        pixels_ref, grad1, grad2, grad3, bias3 = refs[:5]
        refs = refs[5:]
    act1_h, act1_l, act2_h, act2_l, colors, rows, misfit_ref, logit, d3_hl, d2_h, d1_h = refs
    regions, _, segment = rays_ref.shape
    flip = place_ref[0]
    pieces = [(g, s) for g in range(TOGETHER) for s in range(SAMPLES)]
    columns = len(pieces) * segment

    if first:
        grad1[...] = jnp.zeros_like(grad1)
        grad2[...] = jnp.zeros_like(grad2)
        grad3[...] = jnp.zeros_like(grad3)
        bias3[...] = jnp.zeros_like(bias3)
    else:
        grad1[...] = grad1_in[...]
        grad2[...] = grad2_in[...]
        grad3[...] = grad3_in[...]
        bias3[...] = bias3_in[...]
    misfit_ref[...] = jnp.zeros_like(misfit_ref)
    def part(value, g, s):
        start = (g * SAMPLES + s) * segment
        return value[:, start : start + segment]

    def region(step, g):
        return jnp.bitwise_xor(step * TOGETHER + g, flip)

    per = WIDTH // segment
    tiles = columns // WIDTH

    def inputs(step, tile):
        x = [
            rays_ref[region(step, g), s * FEAT : (s + 1) * FEAT, :]
            for g, s in pieces[tile * per : (tile + 1) * per]
        ]
        return split(jnp.concatenate(x, axis=1))

    def at(tile):
        return slice(tile * WIDTH, (tile + 1) * WIDTH)

    def forward(step, cum):
        ones = jnp.ones((ONES, WIDTH), bf16)
        slot = step % 2

        def first_layer(tile):
            xh, xl = inputs(step, tile)
            a1 = jnp.maximum(dot(first_k[...], jnp.concatenate([xh, xl, xh, ones], axis=0)), 0.0)
            a1h, a1l = split(a1)
            act1_h[step, :HIDDEN, at(tile)] = a1h
            act1_h[step, HIDDEN:, at(tile)] = ones
            act1_l[slot, :, at(tile)] = a1l

        def second_layer(tile):
            a1h = act1_h[step, :HIDDEN, at(tile)]
            z2 = dot(second_tk[...], jnp.concatenate([a1h, a1h, act1_l[slot, :, at(tile)]], axis=0))
            a2h, a2l = split(jnp.maximum(z2 + second_b[...], 0.0))
            act2_h[step, :, at(tile)] = a2h
            act2_l[slot, :, at(tile)] = a2l

        def last_layer(tile):
            both = dot(last_thl[...], act2_h[step, :, at(tile)])
            low = dot(last_thl[:OUT_ROWS], act2_l[slot, :, at(tile)])
            raw = both[:OUT_ROWS] + (both[OUT_ROWS:] + low) + last_b[...]
            colors[step, :, at(tile)] = sigmoid(raw[:CHANNELS])
            logit[:, at(tile)] = raw[CHANNELS : CHANNELS + 8]

        for stage in (first_layer, second_layer, last_layer):
            for tile in range(tiles):
                stage(tile)
        t = logit[0:1]
        density = jnp.maximum(t, 0.0) + jnp.log1p(jnp.exp(-jnp.abs(t)))
        slope = sigmoid(t)
        image = misfit_ref[...]
        for g in range(TOGETHER):
            d = region(step, g)
            passed = jnp.exp(-cum)
            before = jnp.ones_like(cum)
            total = jnp.zeros_like(cum)
            rows[step, g, 9:10, :] = passed
            for s in range(SAMPLES):
                i = g * SAMPLES + s
                length = rays_ref[d, SAMPLES * FEAT + s : SAMPLES * FEAT + s + 1, :]
                optical = part(density, g, s) * length
                weight = before * (1.0 - jnp.exp(-optical))
                total = total + optical
                before = jnp.exp(-total)
                image = image + (passed * weight) * colors[step, :, i * segment : (i + 1) * segment]
                rows[step, g, s : s + 1, :] = weight
                rows[step, g, SAMPLES + s : SAMPLES + s + 1, :] = before
                rows[step, g, 2 * SAMPLES + s : 2 * SAMPLES + s + 1, :] = part(slope, g, s) * length
            cum = cum + total
        misfit_ref[...] = image
        return cum

    steps = regions // TOGETHER
    lax.fori_loop(0, steps, forward, jnp.zeros((1, segment), f32), unroll=FORWARD_UNROLL)
    pixels = misfit_ref[...]
    misfit_ref[...] = pixels - target_ref[...]
    if first:
        pixels_ref[...] = pixels
    else:
        pixels_ref[...] = jnp.concatenate([pixels_in[...], pixels], axis=1)

    def backward(turn, behind):
        step = steps - 1 - turn
        misfit = misfit_ref[...]
        slopes = [None] * len(pieces)
        parts = [None] * len(pieces)
        for g in reversed(range(TOGETHER)):
            passed = rows[step, g, 9:10, :]
            later = -behind
            for s in reversed(range(SAMPLES)):
                i = g * SAMPLES + s
                weight = rows[step, g, s : s + 1, :]
                after = rows[step, g, SAMPLES + s : SAMPLES + s + 1, :]
                sc = colors[step, :, i * segment : (i + 1) * segment]
                product = misfit * sc
                value = passed * jnp.sum(product, axis=0, keepdims=True)
                parts[i] = (passed * weight) * (product - product * sc)
                slopes[i] = (value * after + later) * rows[step, g, 2 * SAMPLES + s : 2 * SAMPLES + s + 1, :]
                later = later - weight * value
            behind = -later
        def output(tile):
            mine = slice(tile * per, (tile + 1) * per)
            d3 = jnp.concatenate(
                [
                    jnp.concatenate(parts[mine], axis=1),
                    jnp.concatenate(slopes[mine], axis=1),
                    jnp.zeros((OUT_ROWS - OUT, WIDTH), f32),
                ],
                axis=0,
            )
            high, low = split(d3)
            d3_hl[:OUT_ROWS, at(tile)] = high
            d3_hl[OUT_ROWS:, at(tile)] = low
            bias3[...] += sum(d3[:, i * segment : (i + 1) * segment] for i in range(per))

        def last_layer(tile):
            d3h = d3_hl[:OUT_ROWS, at(tile)]
            d2 = dot(last_k[...], jnp.concatenate([d3h, d3_hl[OUT_ROWS:, at(tile)], d3h], axis=0)).astype(bf16)
            d2_h[:, at(tile)] = jnp.where(act2_h[step, :, at(tile)] > 0, d2, jnp.zeros_like(d2))

        def second_layer(tile):
            high = d2_h[:, at(tile)]
            d1 = dot(second_k[...], jnp.concatenate([high, high], axis=0)).astype(bf16)
            d1_h[:, at(tile)] = jnp.where(act1_h[step, :HIDDEN, at(tile)] > 0, d1, jnp.zeros_like(d1))

        def sum_last():
            grad3[...] += dot_columns(d3_hl[:OUT_ROWS], act2_h[step])

        def sum_second():
            grad2[...] += dot_columns(act1_h[step], d2_h[...])

        def sum_first():
            x = [inputs(step, tile) for tile in range(tiles)]
            xh = jnp.concatenate([h for h, _ in x], axis=1)
            xl = jnp.concatenate([l for _, l in x], axis=1)
            ones = jnp.ones((ONES, columns), bf16)
            both = dot_columns(jnp.concatenate([xh, ones, xl], axis=0), d1_h[...])
            grad1[...] += both[: FEAT + ONES]
            grad1[:FEAT] += both[FEAT + ONES :]

        for stage in (output, last_layer, second_layer):
            for tile in range(tiles):
                stage(tile)
        sum_last()
        sum_second()
        sum_first()
        return behind

    lax.fori_loop(0, steps, backward, jnp.zeros((1, segment), f32), unroll=BACKWARD_UNROLL)
    if not final:
        return

    half = HIDDEN // 2
    third = lax.dot_general(
        jnp.ones((8, segment), f32),
        jnp.concatenate([bias3[...], jnp.zeros((half - OUT_ROWS, segment), f32)], axis=0),
        (((1,), (1,)), ((), ())),
        precision=lax.Precision.HIGHEST,
        preferred_element_type=f32,
    )

    def pack(hidden_ref, others_ref):
        for side in range(2):
            lanes = slice(side * half, (side + 1) * half)
            hidden_ref[side * 256 : side * 256 + 256] = grad2[:HIDDEN, lanes]
            others_ref[side * 32 : 32 + side * 32] = grad1[:FEAT, lanes]
            others_ref[64 + side * 80 : 144 + side * 80] = grad3[:, lanes]
            misc = [grad1[FEAT : FEAT + 1, lanes], grad2[HIDDEN : HIDDEN + 1, lanes], third[0:1]]
            others_ref[224 + side * 8 : 232 + side * 8] = jnp.concatenate(misc + [jnp.zeros((5, half), f32)], axis=0)
        others_ref[240:] = jnp.zeros((PACKED - 240, half), f32)

    @pl.when(place_ref[1] == 0)
    def _():
        pack(keep_ref, send_ref)

    @pl.when(place_ref[1] == 1)
    def _():
        pack(send_ref, keep_ref)


def finish_kernel(place_ref, own_ref, other_ref, first_ref, first_b_ref, second_ref, second_b_ref, last_t_ref, last_b_ref):
    def scale(parts, count):
        squares = sum(jnp.sum(part * part, keepdims=True) for part in parts)
        return 1.0 / jnp.sqrt(squares / count + epsilon)

    def finish(hidden_ref, others_ref):
        def both(ref, start, rows, stride):
            return [ref[start : start + rows, :], ref[start + stride : start + stride + rows, :]]

        parts = both(hidden_ref, 0, 256, 256)
        second_ref[...] = jnp.concatenate(parts, axis=1) * scale(parts, HIDDEN * HIDDEN)
        parts = both(others_ref, 0, 32, 32)
        first_ref[...] = jnp.concatenate(parts, axis=1) * scale(parts, FEAT * HIDDEN)
        parts = both(others_ref, 64, 80, 80)
        last_t_ref[...] = jnp.concatenate(parts, axis=1)[:OUT] * scale(parts, HIDDEN * OUT)
        parts = both(others_ref, 224, 1, 8)
        first_b_ref[...] = jnp.concatenate(parts, axis=1) * scale(parts, HIDDEN)
        parts = both(others_ref, 225, 1, 8)
        second_b_ref[...] = jnp.concatenate(parts, axis=1) * scale(parts, HIDDEN)
        part = others_ref[226:227, :]
        last_b_ref[...] = (part * scale([part], OUT))[:, :OUT]

    @pl.when(place_ref[1] == 0)
    def _():
        finish(own_ref, other_ref)

    @pl.when(place_ref[1] == 1)
    def _():
        finish(other_ref, own_ref)


vmem = pl.BlockSpec(memory_space=pltpu.VMEM)


def shaped(*shape, dtype=f32):
    return jax.ShapeDtypeStruct(shape, dtype)


def prepare_weights(first_weight, first_bias, second_weight, second_bias, last_weight, last_bias):
    return pl.pallas_call(
        weights_kernel,
        in_specs=[vmem] * 6,
        out_specs=[vmem] * 7,
        out_shape=[
            shaped(HIDDEN, 3 * FEAT + ONES, dtype=bf16),
            shaped(HIDDEN, 2 * HIDDEN, dtype=bf16),
            shaped(HIDDEN, 3 * HIDDEN, dtype=bf16),
            shaped(HIDDEN, 1),
            shaped(HIDDEN, 3 * OUT_ROWS, dtype=bf16),
            shaped(2 * OUT_ROWS, HIDDEN, dtype=bf16),
            shaped(OUT_ROWS, 1),
        ],
        compiler_params=pltpu.CompilerParams(vmem_limit_bytes=8 * 2**20),
    )(first_weight, first_bias[None], second_weight, second_bias[None], last_weight.T, last_bias[None])


def step(first, final, place, rays, target, weights, carried):
    regions, _, segment = rays.shape
    columns = TOGETHER * SAMPLES * segment
    steps = regions // TOGETHER
    sums = [
        shaped(FEAT + ONES, HIDDEN),
        shaped(HIDDEN + ONES, HIDDEN),
        shaped(OUT_ROWS, HIDDEN),
        shaped(OUT_ROWS, segment),
    ]
    scratch = [
        pltpu.VMEM((steps, HIDDEN + ONES, columns), bf16),
        pltpu.VMEM((2, HIDDEN, columns), bf16),
        pltpu.VMEM((steps, HIDDEN, columns), bf16),
        pltpu.VMEM((2, HIDDEN, columns), bf16),
        pltpu.VMEM((steps, CHANNELS, columns), f32),
        pltpu.VMEM((steps, TOGETHER, 16, segment), f32),
        pltpu.VMEM((CHANNELS, segment), f32),
        pltpu.VMEM((8, columns), f32),
        pltpu.VMEM((2 * OUT_ROWS, columns), bf16),
        pltpu.VMEM((HIDDEN, columns), bf16),
        pltpu.VMEM((HIDDEN, columns), bf16),
    ]
    width = segment if first else 2 * segment
    if final:
        out_shape = [shaped(CHANNELS, width), shaped(PACKED, 128), shaped(PACKED, 128)]
        scratch = [pltpu.VMEM(s.shape, f32) for s in sums] + scratch
    else:
        out_shape = [shaped(CHANNELS, width)] + sums
    return pl.pallas_call(
        functools.partial(step_kernel, first, final),
        in_specs=[pl.BlockSpec(memory_space=pltpu.SMEM)] + [vmem] * (2 + len(weights) + len(carried)),
        out_specs=[vmem] * len(out_shape),
        out_shape=out_shape,
        scratch_shapes=scratch,
        compiler_params=pltpu.CompilerParams(vmem_limit_bytes=44 * 2**20),
        cost_estimate=pl.CostEstimate(
            flops=2 * 17 * 65536 * steps * columns, bytes_accessed=2**20, transcendentals=0
        ),
    )(place, rays, target, *weights, *carried)


def local(
    features,
    spacing,
    counts,
    depth_rank,
    target,
    first_weight,
    first_bias,
    second_weight,
    second_bias,
    last_weight,
    last_bias,
):
    regions = lax.axis_size("depth")
    chips = regions * lax.axis_size("chip")
    rays = features.shape[-1]
    lanes = rays // regions // PARTS
    place = jnp.stack([jnp.bitwise_xor(depth_rank[0, 0], lax.axis_index("depth")), lax.axis_index("core")])

    got = []
    for i in range(PARTS):
        sent = pl.pallas_call(
            functools.partial(send_kernel, PARTS, i),
            in_specs=[vmem] * 3,
            out_specs=vmem,
            out_shape=shaped(regions, HEIGHT, lanes),
            cost_estimate=pl.CostEstimate(flops=0, bytes_accessed=2**20, transcendentals=0),
        )(
            features[0, 0].transpose(1, 0, 2).reshape(SAMPLES * FEAT, rays),
            spacing[0, 0].reshape(SAMPLES, rays // 128, 128),
            counts[0, 0].reshape(rays // 128, 128),
        )
        got.append(lax.all_to_all(sent, "depth", 0, 0))
    weights = prepare_weights(first_weight, first_bias, second_weight, second_bias, last_weight, last_bias)
    carried = []
    for i in range(PARTS):
        goal = target[0, :, i * lanes : (i + 1) * lanes]
        carried = step(i == 0, i == PARTS - 1, place, got[i], goal, weights, carried)
    pixels, keep, send = carried

    swap = [(0, 1), (1, 0)]
    axes = ("chip", "depth")
    half = keep + lax.ppermute(send, "core", swap)
    shares = lax.all_to_all(half.reshape(chips, PACKED // chips, 128), axes, 0, 0)
    share = jnp.sum(shares, axis=0)
    own = lax.all_to_all(jnp.broadcast_to(share[None], shares.shape), axes, 0, 0).reshape(PACKED, 128)
    other = lax.ppermute(own, "core", swap)
    first_u, first_s, second_u, second_s, last_u, last_s = pl.pallas_call(
        finish_kernel,
        in_specs=[pl.BlockSpec(memory_space=pltpu.SMEM), vmem, vmem],
        out_specs=[vmem] * 6,
        out_shape=[
            shaped(FEAT, HIDDEN),
            shaped(1, HIDDEN),
            shaped(HIDDEN, HIDDEN),
            shaped(1, HIDDEN),
            shaped(OUT, HIDDEN),
            shaped(1, OUT),
        ],
        compiler_params=pltpu.CompilerParams(vmem_limit_bytes=8 * 2**20),
    )(place, own, other)
    return (pixels[None], first_u, first_s[0], second_u, second_s[0], last_u.T, last_s[0])


def solution(mesh):
    views, regions = mesh.devices.shape
    cores = 2
    mesh = Mesh(mesh.devices.reshape(views // cores, cores, regions), ("chip", "core", "depth"))
    view = ("chip", "core")
    return jax.shard_map(
        local,
        mesh=mesh,
        in_specs=(
            P(view, "depth", None, None, None),
            P(view, "depth", None, None),
            P(view, "depth", None),
            P(view, "depth"),
            P(view, None, "depth"),
            P(),
            P(),
            P(),
            P(),
            P(),
            P(),
        ),
        out_specs=(P(view, None, "depth"), P(), P(), P(), P(), P(), P()),
        check_vma=False,
    )
```

```python
import functools

import jax
import jax.numpy as jnp
from jax import lax
from jax.experimental import pallas as pl
from jax.experimental.pallas import tpu as pltpu
from jax.sharding import Mesh
from jax.sharding import PartitionSpec as P

epsilon = 1e-05
f32 = jnp.float32
bf16 = jnp.bfloat16
FEAT, HIDDEN, CHANNELS, SAMPLES = 32, 256, 64, 3
OUT = CHANNELS + 1
OUT_ROWS = 80
ONES = 16
HEIGHT = 104
PARTS = 2
TOGETHER = 4
FORWARD_UNROLL = 2
BACKWARD_UNROLL = 4
WIDTH = 512
PACKED = 512


def split(value):
    high = value.astype(bf16)
    return high, (value - high.astype(f32)).astype(bf16)


def dot(left, right):
    return lax.dot_general(left, right, (((1,), (0,)), ((), ())), preferred_element_type=f32)


def dot_columns(left, right):
    return lax.dot_general(left, right, (((1,), (1,)), ((), ())), preferred_element_type=f32)


def sigmoid(value):
    return 0.5 * jnp.tanh(0.5 * value) + 0.5


def send_kernel(parts, i, features_ref, spacing_ref, counts_ref, sent_ref):
    regions, _, lanes = sent_ref.shape
    wide = lanes // 128
    lengths = [jnp.where(counts_ref[...] > s, spacing_ref[s], 0.0) for s in range(SAMPLES)]
    for j in range(regions):
        start = (j * parts + i) * lanes
        sent_ref[j, : SAMPLES * FEAT, :] = features_ref[:, start : start + lanes]
        row = j * parts * wide
        for k in range(wide if i == 0 else 0):
            sent_ref[j, SAMPLES * FEAT :, k * 128 : (k + 1) * 128] = jnp.concatenate(
                [v[row + q * wide + k : row + q * wide + k + 1] for q in range(parts) for v in lengths]
                + [jnp.zeros((HEIGHT - SAMPLES * (FEAT + parts), 128), f32)],
                axis=0,
            )


def weights_kernel(
    first_ref,
    first_bias_ref,
    second_ref,
    second_bias_ref,
    last_t_ref,
    last_bias_ref,
    first_k,
    second_k,
    second_tk,
    second_b,
    last_k,
    last_thl,
    last_b,
):
    def column(row, size):
        return jnp.transpose(jnp.broadcast_to(row, (8, size)))[:, 0:1]

    high, low = split(jnp.transpose(first_ref[...]))
    bias = column(first_bias_ref[...], HIDDEN)
    bias_h = bias.astype(bf16)
    rest = bias - bias_h.astype(f32)
    bias_m = rest.astype(bf16)
    bias_l = (rest - bias_m.astype(f32)).astype(bf16)
    pad = jnp.zeros((HIDDEN, ONES - 3), bf16)
    first_k[...] = jnp.concatenate([high, high, low, bias_h, bias_m, bias_l, pad], axis=1)
    high, low = split(second_ref[...])
    second_k[...] = jnp.concatenate([high, low], axis=1)
    high, low = split(jnp.transpose(second_ref[...]))
    second_tk[...] = jnp.concatenate([high, low, high], axis=1)
    second_b[...] = column(second_bias_ref[...], HIDDEN)
    last_t = jnp.concatenate([last_t_ref[...], jnp.zeros((128 - OUT, HIDDEN), f32)], axis=0)
    high, low = split(last_t[:OUT_ROWS])
    last_thl[...] = jnp.concatenate([high, low], axis=0)
    high, low = split(jnp.transpose(last_t)[:, :OUT_ROWS])
    last_k[...] = jnp.concatenate([high, high, low], axis=1)
    row = jnp.concatenate([last_bias_ref[...], jnp.zeros((1, 128 - OUT), f32)], axis=1)
    last_b[...] = column(row, 128)[:OUT_ROWS]


def step_kernel(first, final, place_ref, rays_ref, target_ref, *refs):
    first_k, second_k, second_tk, second_b, last_k, last_thl, last_b = refs[:7]
    refs = refs[7:]
    if not first:
        lengths_ref, pixels_in, grad1_in, grad2_in, grad3_in, bias3_in = refs[:6]
        refs = refs[6:]
    else:
        lengths_ref = rays_ref
    top = SAMPLES * FEAT if first else SAMPLES * (FEAT + 1)
    if final:
        pixels_ref, keep_ref, send_ref = refs[:3]
        grad1, grad2, grad3, bias3 = refs[3:7]
        refs = refs[7:]
    else:
        pixels_ref, grad1, grad2, grad3, bias3 = refs[:5]
        refs = refs[5:]
    act1_h, act1_l, act2_h, act2_l, colors, rows, misfit_ref, logit, d3_hl, d2_h, d1_h = refs
    regions, _, segment = rays_ref.shape
    flip = place_ref[0]
    pieces = [(g, s) for g in range(TOGETHER) for s in range(SAMPLES)]
    columns = len(pieces) * segment

    if first:
        grad1[...] = jnp.zeros_like(grad1)
        grad2[...] = jnp.zeros_like(grad2)
        grad3[...] = jnp.zeros_like(grad3)
        bias3[...] = jnp.zeros_like(bias3)
    else:
        grad1[...] = grad1_in[...]
        grad2[...] = grad2_in[...]
        grad3[...] = grad3_in[...]
        bias3[...] = bias3_in[...]
    misfit_ref[...] = jnp.zeros_like(misfit_ref)
    def part(value, g, s):
        start = (g * SAMPLES + s) * segment
        return value[:, start : start + segment]

    def region(step, g):
        return jnp.bitwise_xor(step * TOGETHER + g, flip)

    per = WIDTH // segment
    tiles = columns // WIDTH

    def inputs(step, tile):
        x = [
            rays_ref[region(step, g), s * FEAT : (s + 1) * FEAT, :]
            for g, s in pieces[tile * per : (tile + 1) * per]
        ]
        return split(jnp.concatenate(x, axis=1))

    def at(tile):
        return slice(tile * WIDTH, (tile + 1) * WIDTH)

    def forward(step, cum):
        ones = jnp.ones((ONES, WIDTH), bf16)
        slot = step % 2

        def first_layer(tile):
            xh, xl = inputs(step, tile)
            a1 = jnp.maximum(dot(first_k[...], jnp.concatenate([xh, xl, xh, ones], axis=0)), 0.0)
            a1h, a1l = split(a1)
            act1_h[step, :HIDDEN, at(tile)] = a1h
            act1_h[step, HIDDEN:, at(tile)] = ones
            act1_l[slot, :, at(tile)] = a1l

        def second_layer(tile):
            a1h = act1_h[step, :HIDDEN, at(tile)]
            z2 = dot(second_tk[...], jnp.concatenate([a1h, a1h, act1_l[slot, :, at(tile)]], axis=0))
            a2h, a2l = split(jnp.maximum(z2 + second_b[...], 0.0))
            act2_h[step, :, at(tile)] = a2h
            act2_l[slot, :, at(tile)] = a2l

        def last_layer(tile):
            both = dot(last_thl[...], act2_h[step, :, at(tile)])
            low = dot(last_thl[:OUT_ROWS], act2_l[slot, :, at(tile)])
            raw = both[:OUT_ROWS] + (both[OUT_ROWS:] + low) + last_b[...]
            colors[step, :, at(tile)] = sigmoid(raw[:CHANNELS])
            logit[:, at(tile)] = raw[CHANNELS : CHANNELS + 8]

        for stage in (first_layer, second_layer, last_layer):
            for tile in range(tiles):
                stage(tile)
        t = logit[0:1]
        density = jnp.maximum(t, 0.0) + jnp.log1p(jnp.exp(-jnp.abs(t)))
        slope = sigmoid(t)
        image = misfit_ref[...]
        for g in range(TOGETHER):
            d = region(step, g)
            passed = jnp.exp(-cum)
            before = jnp.ones_like(cum)
            total = jnp.zeros_like(cum)
            rows[step, g, 9:10, :] = passed
            for s in range(SAMPLES):
                i = g * SAMPLES + s
                length = lengths_ref[d, top + s : top + s + 1, :]
                optical = part(density, g, s) * length
                weight = before * (1.0 - jnp.exp(-optical))
                total = total + optical
                before = jnp.exp(-total)
                image = image + (passed * weight) * colors[step, :, i * segment : (i + 1) * segment]
                rows[step, g, s : s + 1, :] = weight
                rows[step, g, SAMPLES + s : SAMPLES + s + 1, :] = before
                rows[step, g, 2 * SAMPLES + s : 2 * SAMPLES + s + 1, :] = part(slope, g, s) * length
            cum = cum + total
        misfit_ref[...] = image
        return cum

    steps = regions // TOGETHER
    lax.fori_loop(0, steps, forward, jnp.zeros((1, segment), f32), unroll=FORWARD_UNROLL)
    pixels = misfit_ref[...]
    misfit_ref[...] = pixels - target_ref[...]
    if first:
        pixels_ref[...] = pixels
    else:
        pixels_ref[...] = jnp.concatenate([pixels_in[...], pixels], axis=1)

    def backward(turn, behind):
        step = steps - 1 - turn
        misfit = misfit_ref[...]
        slopes = [None] * len(pieces)
        parts = [None] * len(pieces)
        for g in reversed(range(TOGETHER)):
            passed = rows[step, g, 9:10, :]
            later = -behind
            for s in reversed(range(SAMPLES)):
                i = g * SAMPLES + s
                weight = rows[step, g, s : s + 1, :]
                after = rows[step, g, SAMPLES + s : SAMPLES + s + 1, :]
                sc = colors[step, :, i * segment : (i + 1) * segment]
                product = misfit * sc
                value = passed * jnp.sum(product, axis=0, keepdims=True)
                parts[i] = (passed * weight) * (product - product * sc)
                slopes[i] = (value * after + later) * rows[step, g, 2 * SAMPLES + s : 2 * SAMPLES + s + 1, :]
                later = later - weight * value
            behind = -later
        def output(tile):
            mine = slice(tile * per, (tile + 1) * per)
            d3 = jnp.concatenate(
                [
                    jnp.concatenate(parts[mine], axis=1),
                    jnp.concatenate(slopes[mine], axis=1),
                    jnp.zeros((OUT_ROWS - OUT, WIDTH), f32),
                ],
                axis=0,
            )
            high, low = split(d3)
            d3_hl[:OUT_ROWS, at(tile)] = high
            d3_hl[OUT_ROWS:, at(tile)] = low
            bias3[...] += sum(d3[:, i * segment : (i + 1) * segment] for i in range(per))

        def last_layer(tile):
            d3h = d3_hl[:OUT_ROWS, at(tile)]
            d2 = dot(last_k[...], jnp.concatenate([d3h, d3_hl[OUT_ROWS:, at(tile)], d3h], axis=0)).astype(bf16)
            d2_h[:, at(tile)] = jnp.where(act2_h[step, :, at(tile)] > 0, d2, jnp.zeros_like(d2))

        def second_layer(tile):
            high = d2_h[:, at(tile)]
            d1 = dot(second_k[...], jnp.concatenate([high, high], axis=0)).astype(bf16)
            d1_h[:, at(tile)] = jnp.where(act1_h[step, :HIDDEN, at(tile)] > 0, d1, jnp.zeros_like(d1))

        def sum_last():
            grad3[...] += dot_columns(d3_hl[:OUT_ROWS], act2_h[step])

        def sum_second():
            grad2[...] += dot_columns(act1_h[step], d2_h[...])

        def sum_first():
            x = [inputs(step, tile) for tile in range(tiles)]
            xh = jnp.concatenate([h for h, _ in x], axis=1)
            xl = jnp.concatenate([l for _, l in x], axis=1)
            ones = jnp.ones((ONES, columns), bf16)
            both = dot_columns(jnp.concatenate([xh, ones, xl], axis=0), d1_h[...])
            grad1[...] += both[: FEAT + ONES]
            grad1[:FEAT] += both[FEAT + ONES :]

        for stage in (output, last_layer, second_layer):
            for tile in range(tiles):
                stage(tile)
        sum_last()
        sum_second()
        sum_first()
        return behind

    lax.fori_loop(0, steps, backward, jnp.zeros((1, segment), f32), unroll=BACKWARD_UNROLL)
    if not final:
        return

    half = HIDDEN // 2
    third = lax.dot_general(
        jnp.ones((8, segment), f32),
        jnp.concatenate([bias3[...], jnp.zeros((half - OUT_ROWS, segment), f32)], axis=0),
        (((1,), (1,)), ((), ())),
        precision=lax.Precision.HIGHEST,
        preferred_element_type=f32,
    )

    def pack(hidden_ref, others_ref):
        for side in range(2):
            lanes = slice(side * half, (side + 1) * half)
            hidden_ref[side * 256 : side * 256 + 256] = grad2[:HIDDEN, lanes]
            others_ref[side * 32 : 32 + side * 32] = grad1[:FEAT, lanes]
            others_ref[64 + side * 80 : 144 + side * 80] = grad3[:, lanes]
            misc = [grad1[FEAT : FEAT + 1, lanes], grad2[HIDDEN : HIDDEN + 1, lanes], third[0:1]]
            others_ref[224 + side * 8 : 232 + side * 8] = jnp.concatenate(misc + [jnp.zeros((5, half), f32)], axis=0)
        others_ref[240:] = jnp.zeros((PACKED - 240, half), f32)

    @pl.when(place_ref[1] == 0)
    def _():
        pack(keep_ref, send_ref)

    @pl.when(place_ref[1] == 1)
    def _():
        pack(send_ref, keep_ref)


def finish_kernel(place_ref, own_ref, other_ref, first_ref, first_b_ref, second_ref, second_b_ref, last_t_ref, last_b_ref):
    def scale(parts, count):
        squares = sum(jnp.sum(part * part, keepdims=True) for part in parts)
        return 1.0 / jnp.sqrt(squares / count + epsilon)

    def finish(hidden_ref, others_ref):
        def both(ref, start, rows, stride):
            return [ref[start : start + rows, :], ref[start + stride : start + stride + rows, :]]

        parts = both(hidden_ref, 0, 256, 256)
        second_ref[...] = jnp.concatenate(parts, axis=1) * scale(parts, HIDDEN * HIDDEN)
        parts = both(others_ref, 0, 32, 32)
        first_ref[...] = jnp.concatenate(parts, axis=1) * scale(parts, FEAT * HIDDEN)
        parts = both(others_ref, 64, 80, 80)
        last_t_ref[...] = jnp.concatenate(parts, axis=1)[:OUT] * scale(parts, HIDDEN * OUT)
        parts = both(others_ref, 224, 1, 8)
        first_b_ref[...] = jnp.concatenate(parts, axis=1) * scale(parts, HIDDEN)
        parts = both(others_ref, 225, 1, 8)
        second_b_ref[...] = jnp.concatenate(parts, axis=1) * scale(parts, HIDDEN)
        part = others_ref[226:227, :]
        last_b_ref[...] = (part * scale([part], OUT))[:, :OUT]

    @pl.when(place_ref[1] == 0)
    def _():
        finish(own_ref, other_ref)

    @pl.when(place_ref[1] == 1)
    def _():
        finish(other_ref, own_ref)


vmem = pl.BlockSpec(memory_space=pltpu.VMEM)


def shaped(*shape, dtype=f32):
    return jax.ShapeDtypeStruct(shape, dtype)


def prepare_weights(first_weight, first_bias, second_weight, second_bias, last_weight, last_bias):
    return pl.pallas_call(
        weights_kernel,
        in_specs=[vmem] * 6,
        out_specs=[vmem] * 7,
        out_shape=[
            shaped(HIDDEN, 3 * FEAT + ONES, dtype=bf16),
            shaped(HIDDEN, 2 * HIDDEN, dtype=bf16),
            shaped(HIDDEN, 3 * HIDDEN, dtype=bf16),
            shaped(HIDDEN, 1),
            shaped(HIDDEN, 3 * OUT_ROWS, dtype=bf16),
            shaped(2 * OUT_ROWS, HIDDEN, dtype=bf16),
            shaped(OUT_ROWS, 1),
        ],
        compiler_params=pltpu.CompilerParams(vmem_limit_bytes=8 * 2**20),
    )(first_weight, first_bias[None], second_weight, second_bias[None], last_weight.T, last_bias[None])


def step(first, final, place, rays, target, weights, carried):
    regions, _, segment = rays.shape
    columns = TOGETHER * SAMPLES * segment
    steps = regions // TOGETHER
    sums = [
        shaped(FEAT + ONES, HIDDEN),
        shaped(HIDDEN + ONES, HIDDEN),
        shaped(OUT_ROWS, HIDDEN),
        shaped(OUT_ROWS, segment),
    ]
    scratch = [
        pltpu.VMEM((steps, HIDDEN + ONES, columns), bf16),
        pltpu.VMEM((2, HIDDEN, columns), bf16),
        pltpu.VMEM((steps, HIDDEN, columns), bf16),
        pltpu.VMEM((2, HIDDEN, columns), bf16),
        pltpu.VMEM((steps, CHANNELS, columns), f32),
        pltpu.VMEM((steps, TOGETHER, 16, segment), f32),
        pltpu.VMEM((CHANNELS, segment), f32),
        pltpu.VMEM((8, columns), f32),
        pltpu.VMEM((2 * OUT_ROWS, columns), bf16),
        pltpu.VMEM((HIDDEN, columns), bf16),
        pltpu.VMEM((HIDDEN, columns), bf16),
    ]
    width = segment if first else 2 * segment
    if final:
        out_shape = [shaped(CHANNELS, width), shaped(PACKED, 128), shaped(PACKED, 128)]
        scratch = [pltpu.VMEM(s.shape, f32) for s in sums] + scratch
    else:
        out_shape = [shaped(CHANNELS, width)] + sums
    return pl.pallas_call(
        functools.partial(step_kernel, first, final),
        in_specs=[pl.BlockSpec(memory_space=pltpu.SMEM)] + [vmem] * (2 + len(weights) + len(carried)),
        out_specs=[vmem] * len(out_shape),
        out_shape=out_shape,
        scratch_shapes=scratch,
        compiler_params=pltpu.CompilerParams(vmem_limit_bytes=44 * 2**20),
        cost_estimate=pl.CostEstimate(
            flops=2 * 17 * 65536 * steps * columns, bytes_accessed=2**20, transcendentals=0
        ),
    )(place, rays, target, *weights, *carried)


def local(
    features,
    spacing,
    counts,
    depth_rank,
    target,
    first_weight,
    first_bias,
    second_weight,
    second_bias,
    last_weight,
    last_bias,
):
    regions = lax.axis_size("depth")
    chips = regions * lax.axis_size("chip")
    rays = features.shape[-1]
    lanes = rays // regions // PARTS
    place = jnp.stack([jnp.bitwise_xor(depth_rank[0, 0], lax.axis_index("depth")), lax.axis_index("core")])

    got = []
    for i in range(PARTS):
        sent = pl.pallas_call(
            functools.partial(send_kernel, PARTS, i),
            in_specs=[vmem] * 3,
            out_specs=vmem,
            out_shape=shaped(regions, HEIGHT if i == 0 else SAMPLES * FEAT, lanes),
            cost_estimate=pl.CostEstimate(flops=0, bytes_accessed=2**20, transcendentals=0),
        )(
            features[0, 0].transpose(1, 0, 2).reshape(SAMPLES * FEAT, rays),
            spacing[0, 0].reshape(SAMPLES, rays // 128, 128),
            counts[0, 0].reshape(rays // 128, 128),
        )
        got.append(lax.all_to_all(sent, "depth", 0, 0))
    weights = prepare_weights(first_weight, first_bias, second_weight, second_bias, last_weight, last_bias)
    carried = []
    for i in range(PARTS):
        goal = target[0, :, i * lanes : (i + 1) * lanes]
        carried = step(i == 0, i == PARTS - 1, place, got[i], goal, weights, [got[0], *carried] if i else [])
    pixels, keep, send = carried

    swap = [(0, 1), (1, 0)]
    axes = ("chip", "depth")
    half = keep + lax.ppermute(send, "core", swap)
    shares = lax.all_to_all(half.reshape(chips, PACKED // chips, 128), axes, 0, 0)
    share = jnp.sum(shares, axis=0)
    own = lax.all_to_all(jnp.broadcast_to(share[None], shares.shape), axes, 0, 0).reshape(PACKED, 128)
    other = lax.ppermute(own, "core", swap)
    first_u, first_s, second_u, second_s, last_u, last_s = pl.pallas_call(
        finish_kernel,
        in_specs=[pl.BlockSpec(memory_space=pltpu.SMEM), vmem, vmem],
        out_specs=[vmem] * 6,
        out_shape=[
            shaped(FEAT, HIDDEN),
            shaped(1, HIDDEN),
            shaped(HIDDEN, HIDDEN),
            shaped(1, HIDDEN),
            shaped(OUT, HIDDEN),
            shaped(1, OUT),
        ],
        compiler_params=pltpu.CompilerParams(vmem_limit_bytes=8 * 2**20),
    )(place, own, other)
    return (pixels[None], first_u, first_s[0], second_u, second_s[0], last_u.T, last_s[0])


def solution(mesh):
    views, regions = mesh.devices.shape
    cores = 2
    mesh = Mesh(mesh.devices.reshape(views // cores, cores, regions), ("chip", "core", "depth"))
    view = ("chip", "core")
    return jax.shard_map(
        local,
        mesh=mesh,
        in_specs=(
            P(view, "depth", None, None, None),
            P(view, "depth", None, None),
            P(view, "depth", None),
            P(view, "depth"),
            P(view, None, "depth"),
            P(),
            P(),
            P(),
            P(),
            P(),
            P(),
        ),
        out_specs=(P(view, None, "depth"), P(), P(), P(), P(), P(), P()),
        check_vma=False,
    )
```
